128 devices in a mesh: gz: 4 (over z), gx: 32 (over y, x, core).
Axes of the slice: x: 4, y: 4, z: 4, core: 2. Of those that a mesh axis runs over, the one named last changes fastest.
Arguments:
- features: bfloat16 [4, 6144, 6144], P('gz', 'gx'), may hold values from -6 to 6
- active_count: int32 [4, 32], P('gz', 'gx'), may hold values from 48 to 192, as said below
- neighbors: int32 [4, 27, 6144], P('gz', None, 'gx'), may hold values from -1 to 623, as said below
- owner: int32 [4, 6144], P('gz', 'gx'), may hold values from 0 to 127, as said below
- arrival_cell: int32 [4, 12288], P('gz', 'gx'), may hold values from -1 to 191, as said below
- w_enc: bfloat16 [27, 96, 96], replicated, may hold values from -0.125 to 0.125
- w_down: bfloat16 [768, 96], replicated, may hold values from -0.21875 to 0.21875
- w_mid: bfloat16 [27, 96, 96], replicated, may hold values from -0.125 to 0.125
- w_up: bfloat16 [96, 768], replicated, may hold values from -0.625 to 0.625
- w_dec: bfloat16 [27, 96, 96], replicated, may hold values from -0.125 to 0.125
Outputs:
- decoded: bfloat16 [4, 6144, 6144], P('gz', 'gx')
The draws below stay inside these ranges and needn't reach their ends.
Inputs may be any that keep to these rules, and one draw needn't show every extreme that they name: `active_count`: at least 48; some device has exactly 192 active bricks and some exactly 48. `neighbors`: -1 means no brick at that offset; a value n below 192 names brick n of the same device; a value n of 192 or more names boundary brick (n - 192) % 48 of the neighbouring device given in the reference program. Every device sends either no brick or exactly 3 bricks to each owner, and every owner receives exactly 192 bricks in all. `arrival_cell`: row o, slot s * 3 + r is the cell of the r-th brick (in brick order) that device s sends to owner o, or -1 if s sends none to o; each owner's cells 0 to 191 each occur once.
All inputs are finite; a program needn't handle non-finite values.
Results may differ from the reference program's by a relative error of at most 0.0095.
Values may be sent and summed in bfloat16 or wider, within the bound.
A program may use at most 128 MiB of HBM per device.

```python
import jax
import jax.numpy as jnp
from jax import lax

C = 96
K = 27
BR = 192
HB = 48
CB = 24
CAP = 3
SLOTS = 384
N_GZ = 4
N_GX = 32
DEVICES = 128


def route_plan(key):
    keys = jax.random.split(key, 3)
    groups = BR // CAP
    shuffled = jax.random.permutation(keys[0], DEVICES).astype(jnp.int32)
    forced = (shuffled == 1) | (shuffled == DEVICES // 2) | (shuffled == DEVICES - 1)
    score = jnp.where(forced, 0, 1).astype(jnp.int32)
    ordering = jnp.argsort(score, stable=True)
    offsets = shuffled[ordering][:groups].astype(jnp.int32)
    order = jax.vmap(lambda k: jax.random.permutation(k, BR))(jax.random.split(keys[1], DEVICES)).astype(jnp.int32)
    group = order // CAP
    device = jnp.arange(DEVICES, dtype=jnp.int32)[:, None]
    owners = (device + offsets[group]) % DEVICES
    cells = jax.vmap(lambda k: jax.random.permutation(k, BR))(jax.random.split(keys[2], DEVICES)).astype(jnp.int32)
    receiver = jnp.arange(DEVICES, dtype=jnp.int32)[:, None, None]
    sender = (receiver - offsets[None, :, None]) % DEVICES
    where_to = sender * CAP + jnp.arange(CAP, dtype=jnp.int32)[None, None, :]
    values = cells.reshape(DEVICES, groups, CAP)
    receiver_all = jnp.broadcast_to(receiver, where_to.shape)
    arrivals = jnp.full((DEVICES, SLOTS), -1, jnp.int32).at[receiver_all, where_to].set(values)
    return (owners.reshape(N_GZ, N_GX * BR), arrivals.reshape(N_GZ, N_GX * SLOTS))


def draw_owner(key, part):
    owners = route_plan(key)[0]
    return owners


def draw_arrival_cell(key, part):
    arrivals = route_plan(key)[1]
    return arrivals


def draw_neighbors(key, part):
    key = jax.random.fold_in(key, 3)
    keys = jax.random.split(key, 4)
    shape = (N_GZ, K, N_GX * BR)
    kind = jax.random.randint(keys[0], shape, 0, 10)
    local = jax.random.randint(keys[1], shape, 0, BR)
    direction = jax.random.randint(keys[2], shape, 0, 8)
    direction = direction + (direction >= 4).astype(jnp.int32)
    side = jax.random.randint(keys[3], shape, 0, HB)
    remote = BR + direction * HB + side
    values = jnp.where(kind < 2, -1, jnp.where(kind < 7, local, remote)).astype(jnp.int32)
    values = values.at[0, 0, 0].set(-1)
    values = values.at[0, 1, 0].set(BR + 9 * HB - 1)
    return values


def draw_active_count(key, part):
    key = jax.random.fold_in(key, 5)
    keys = jax.random.split(key, 3)
    counts = jax.random.randint(keys[0], (DEVICES,), BR // 4, BR + 1)
    highest = jax.random.randint(keys[1], (), 0, DEVICES)
    lowest = (highest + 1 + jax.random.randint(keys[2], (), 0, DEVICES - 1)) % DEVICES
    counts = counts.at[highest].set(BR).at[lowest].set(BR // 4)
    return counts.reshape(N_GZ, N_GX).astype(jnp.int32)


def block_scale(key, shape, pieces, smallest, top_value):
    def one(dim, blocks):
        draws = jax.random.uniform(jax.random.fold_in(jax.random.fold_in(key, 6), dim), (blocks,), jnp.float32, smallest / len(pieces), top_value / len(pieces))
        return jnp.repeat(jnp.exp(draws), shape[dim] // blocks).reshape((-1,) + (1,) * (len(shape) - dim - 1))

    level = one(*pieces[0])
    for cut in pieces[1:]:
        level = level * one(*cut)
    return level


def noise(stream_key, extent, width, most, cuts=(), kind=jnp.bfloat16):
    values = jax.random.normal(stream_key, extent, jnp.float32) * width
    if len(cuts) > 0:
        values = block_scale(stream_key, extent, cuts, -0.22, 0.18) * values
    return jnp.clip(values, min=-most, max=most).astype(kind)


def setup_inputs(seed: int = 0) -> dict:
    key_list = jax.random.split(jax.random.key(seed), 11)
    features = noise(key_list[0], (N_GZ, N_GX * BR, 64 * C), 1.0, 6.0, ((0, 4), (1, 32)))
    active_count = draw_active_count(jax.random.fold_in(key_list[10], 71), 0)
    neighbors = draw_neighbors(jax.random.fold_in(key_list[10], 71), 0)
    owner = draw_owner(jax.random.fold_in(key_list[10], 71), 0)
    arrival_cell = draw_arrival_cell(jax.random.fold_in(key_list[10], 71), 0)
    w_enc = noise(key_list[5], (K, C, C), (K * C) ** -0.5, 0.125)
    w_down = noise(key_list[6], (8 * C, C), (8 * C) ** -0.5, 0.21875)
    w_mid = noise(key_list[7], (K, C, C), (K * C) ** -0.5, 0.125)
    w_up = noise(key_list[8], (C, 8 * C), C ** -0.5, 0.625)
    w_dec = noise(key_list[9], (K, C, C), (K * C) ** -0.5, 0.125)
    return {"features": features, "active_count": active_count, "neighbors": neighbors, "owner": owner, "arrival_cell": arrival_cell, "w_enc": w_enc, "w_down": w_down, "w_mid": w_mid, "w_up": w_up, "w_dec": w_dec}


def to_cells(vox, chans):
    count = vox.shape[0]
    parts = vox.reshape(count, 2, 2, 2, 2, 2, 2, chans).transpose(0, 1, 3, 5, 2, 4, 6, 7)
    return parts.reshape(count, 8, 8 * chans)


def from_cells(cells, chans):
    count = cells.shape[0]
    parts = cells.reshape(count, 2, 2, 2, 2, 2, 2, chans).transpose(0, 1, 4, 2, 5, 3, 6, 7)
    return parts.reshape(count, 64, chans)


def coarse_mix(vox, weight):
    chans = weight.shape[1]
    padded = jnp.pad(vox, ((0, 0), (1, 1), (1, 1), (1, 1), (0, 0)))
    total = jnp.zeros((vox.shape[0] * 64, chans), jnp.float32)
    for dz in range(3):
        for dy in range(3):
            for dx in range(3):
                piece = padded[:, dz:dz + 4, dy:dy + 4, dx:dx + 4].reshape(-1, chans)
                total = total + jnp.dot(piece, weight[(dz * 3 + dy) * 3 + dx], preferred_element_type=jnp.float32)
    return total


def fine_conv(field, table, weight):
    faces = field[:, :, :HB]
    padded = jnp.pad(faces, ((1, 1), (1, 1), (0, 0), (0, 0)))
    blank = jnp.zeros((), jnp.bfloat16)

    def one_device(index):
        layer = index // N_GX
        slab = index % N_GX
        own = field[layer, slab]
        zero = jnp.zeros((), jnp.int32)
        cycle = lax.dynamic_slice(padded, (layer, slab, zero, zero), (3, 3, HB, 64 * C)).reshape(9 * HB, 64 * C)
        extended = jnp.concatenate([own, cycle], axis=0)
        rows = table[layer, :, slab]
        total = jnp.zeros((BR * 64, C), jnp.float32)
        for k in range(K):
            picked = jnp.take(extended, jnp.maximum(rows[k], 0), axis=0)
            picked = jnp.where((rows[k] >= 0)[:, None], picked, blank)
            total = total + jnp.dot(picked.reshape(BR * 64, C), weight[k], preferred_element_type=jnp.float32)
        return total

    result = lax.map(one_device, jnp.arange(DEVICES, dtype=jnp.int32))
    return result.reshape(N_GZ, N_GX, BR, 64 * C)


def reference(features, active_count, neighbors, owner, arrival_cell, w_enc, w_down, w_mid, w_up, w_dec):
    blank = jnp.zeros((), jnp.bfloat16)
    field = features.reshape(N_GZ, N_GX, BR, 64 * C)
    live = (jnp.arange(BR, dtype=jnp.int32)[None, None, :] < active_count[:, :, None])[..., None]
    x0 = jnp.where(live, field, blank)
    table = neighbors.reshape(N_GZ, K, N_GX, BR)
    conv_one = fine_conv(x0, table, w_enc)
    encoded = jnp.where(live, x0.astype(jnp.float32) + jax.nn.relu(conv_one), 0.0).astype(jnp.bfloat16)
    cells = to_cells(encoded.reshape(DEVICES * BR, 64, C), C)
    pooled = jnp.dot(cells.reshape(-1, 8 * C), w_down, preferred_element_type=jnp.float32)
    pooled = pooled.reshape(N_GZ, N_GX, BR, 8 * C)
    pooled = jnp.where(live, pooled, 0.0).astype(jnp.bfloat16).reshape(DEVICES * BR, 8 * C)
    owners = owner.reshape(DEVICES, BR)
    later = jnp.arange(BR, dtype=jnp.int32)[None, :] < jnp.arange(BR, dtype=jnp.int32)[:, None]
    same = owners[:, :, None] == owners[:, None, :]
    rank = jnp.sum(jnp.logical_and(same, later[None]).astype(jnp.int32), axis=2).astype(jnp.int32)
    source = jnp.arange(DEVICES, dtype=jnp.int32)[:, None]
    arrivals = arrival_cell.reshape(DEVICES, SLOTS)
    cell = arrivals[owners, source * CAP + rank]
    place = (owners * BR + cell).reshape(-1).astype(jnp.int32)
    coarse = jnp.zeros((DEVICES * BR, 8 * C), jnp.bfloat16).at[place].set(pooled)
    bricks = from_cells(coarse.reshape(DEVICES * CB, 8, 8 * C), C).reshape(DEVICES, CB, 4, 4, 4, C)

    def mix_device(vox):
        mixed = coarse_mix(vox, w_mid).reshape(CB, 4, 4, 4, C)
        return (vox.astype(jnp.float32) + jax.nn.relu(mixed)).astype(jnp.bfloat16)

    middle = lax.map(mix_device, bricks)
    middle_cells = to_cells(middle.reshape(DEVICES * CB, 64, C), C).reshape(DEVICES * BR, 8 * C)
    back = middle_cells[place]
    lifted = jnp.dot(back.reshape(DEVICES * BR * 8, C), w_up, preferred_element_type=jnp.float32)
    lifted = from_cells(lifted.reshape(DEVICES * BR, 8, 8 * C), C).reshape(N_GZ, N_GX, BR, 64 * C)
    restored = jnp.where(live, encoded.astype(jnp.float32) + lifted, 0.0).astype(jnp.bfloat16)
    conv_two = fine_conv(restored, table, w_dec)
    decoded = jnp.where(live, restored.astype(jnp.float32) + jax.nn.relu(conv_two), 0.0).astype(jnp.bfloat16)
    return decoded.reshape(N_GZ, N_GX * BR, 64 * C)
```

```python
import functools

import jax
import jax.numpy as jnp
from jax import lax
from jax.experimental import pallas as pl
from jax.experimental.pallas import tpu as pltpu
from jax.sharding import PartitionSpec as P


ORDER = [[(q - i) % 4 for q in range(4)] for i in range(4)]
CUT = (96, 64, 32)

def conv_kernel(nb, chunks, staged, table, count, w_ref, own_hbm, halo_hbm, out_ref, rot, gbuf, sem):
    step = pl.program_id(0)
    bricks = own_hbm.shape[0]
    total = bricks + halo_hbm.shape[0]
    lane = lax.broadcasted_iota(jnp.int32, (16, 128), 1)

    @pl.when(step == 0)
    def _():
        a = pltpu.make_async_copy(own_hbm, rot.at[0, pl.ds(0, bricks)], sem.at[0])
        b = pltpu.make_async_copy(halo_hbm, rot.at[0, pl.ds(bricks, total - bricks)], sem.at[1])
        a.start(); b.start();
        for j in range(4):
            rot[j, total] = jnp.zeros((3, 16, 128), jnp.bfloat16)
        a.wait(); b.wait()
        def rotate(n, c):
            tiles = [rot[0, n, t] for t in range(3)]
            for j in range(1, 4):
                amount = (96 * j) % 128
                rolled = [pltpu.roll(x.astype(jnp.float32), amount, 1).astype(jnp.bfloat16) for x in tiles]
                for u in range(3):
                    hi = (128 * u + 127 - 96 * j) // 128 % 3
                    lo = (128 * u - 96 * j) // 128 % 3
                    edge = amount
                    rot[j, n, u] = jnp.where(lane >= edge, rolled[hi], rolled[lo])
            return c
        lax.fori_loop(0, total, rotate, 0, unroll=8)

    def gather(c, b):
        base = (step * nb + b) * 28
        lanes = [[] for _ in range(4)]
        for g in chunks[c]:
            loads = [[rot[j, table[base + 4 * g + j], t] for t in range(3)] for j in range(4)]
            for i in range(4):
                for u in range(3):
                    lanes[i].append(jnp.where(lane < CUT[u], loads[ORDER[i][u]][u], loads[ORDER[i][u + 1]][u]))
        return lanes

    acc = [None] * 4
    for c in range(len(chunks)):
        got = [gather(c, b) for b in range(nb)]
        for i in range(4):
            if staged:
                for b in range(nb):
                    for u, x in enumerate(got[b][i]):
                        gbuf[c % 2, i, b * 16:(b + 1) * 16, u * 128:(u + 1) * 128] = x
                lhs = gbuf[c % 2, i, :, :128 * 3 * len(chunks[c])]
            else:
                lhs = jnp.concatenate([jnp.concatenate(got[b][i], axis=1) for b in range(nb)], axis=0)
            pieces = []
            for g in chunks[c]:
                for q in range(4):
                    k = 4 * g + ORDER[i][q]
                    pieces.append(w_ref[k] if k < 27 else jnp.zeros((96, 128), jnp.bfloat16))
            rhs = jnp.concatenate(pieces, axis=0)
            part = jnp.dot(lhs, rhs, preferred_element_type=jnp.float32)
            acc[i] = part if acc[i] is None else acc[i] + part
    r1 = pltpu.roll(acc[1], 96, 1)
    r2 = pltpu.roll(acc[2], 64, 1)
    r3 = pltpu.roll(acc[3], 32, 1)
    rows = lax.broadcasted_iota(jnp.int32, (nb * 16, 128), 0) // 16 + step * nb
    lanes = lax.broadcasted_iota(jnp.int32, (nb * 16, 128), 1)
    live = rows < count[0]
    tiles = (jnp.where(lanes < 96, acc[0], r1), jnp.where(lanes < 64, r1, r2), jnp.where(lanes < 32, r2, r3))
    for u in range(3):
        own = rot[0, pl.ds(step * nb, nb), u].reshape(nb * 16, 128).astype(jnp.float32)
        val = jnp.where(live, own + jnp.maximum(tiles[u], 0.0), 0.0).astype(jnp.bfloat16)
        out_ref[:, u] = val.reshape(nb, 16, 128)

def conv(table, count, w, own, halo, nb=16, chunks=((0,1),(2,3),(4,5),(6,)), staged=False):
    bricks = own.shape[0]
    total = bricks + halo.shape[0]
    kc = max(len(c) for c in chunks) * 384
    return pl.pallas_call(
        functools.partial(conv_kernel, nb, chunks, staged),
        grid=(bricks // nb,),
        out_shape=jax.ShapeDtypeStruct((bricks, 3, 16, 128), jnp.bfloat16),
        in_specs=[pl.BlockSpec(memory_space=pltpu.SMEM), pl.BlockSpec(memory_space=pltpu.SMEM),
                  pl.BlockSpec((27, 96, 128), lambda s: (0, 0, 0)),
                  pl.BlockSpec(memory_space=pl.ANY), pl.BlockSpec(memory_space=pl.ANY)],
        out_specs=pl.BlockSpec((nb, 3, 16, 128), lambda s: (s, 0, 0, 0)),
        scratch_shapes=[pltpu.VMEM((4, total + 1, 3, 16, 128), jnp.bfloat16),
                        pltpu.VMEM((2, 4, nb * 16, kc), jnp.bfloat16) if staged else pltpu.VMEM((8, 128), jnp.float32),
                        pltpu.SemaphoreType.DMA((2,))],
        compiler_params=pltpu.CompilerParams(vmem_limit_bytes=56 * 1024 * 1024),
        name="conv",
    )(table, count, w, own, halo)

def dense(x):
    return x.reshape(x.shape[0], 16, 3, 128).transpose(0, 2, 1, 3)
def undense(x):
    return x.transpose(0, 2, 1, 3).reshape(x.shape[0], 6144)


def padded_2(block, sides, width):
    for axis, dim in sides:
        count = lax.axis_size(axis)
        forward = [(i, i + 1) for i in range(count - 1)]
        backward = [(target, source) for source, target in forward]
        low = lax.ppermute(
            lax.slice_in_dim(block, block.shape[dim] - width, None, axis=dim), axis, forward
        )
        high = lax.ppermute(lax.slice_in_dim(block, 0, width, axis=dim), axis, backward)
        block = jnp.concatenate([low, block, high], axis=dim)
    return block


def to_cells(vox, chans):
    count = vox.shape[0]
    parts = vox.reshape(count, 2, 2, 2, 2, 2, 2, chans).transpose(0, 1, 3, 5, 2, 4, 6, 7)
    return parts.reshape(count, 8, 8 * chans)


def from_cells(cells, chans):
    count = cells.shape[0]
    parts = cells.reshape(count, 2, 2, 2, 2, 2, 2, chans).transpose(0, 1, 4, 2, 5, 3, 6, 7)
    return parts.reshape(count, 64, chans)


def coarse_mix(vox, weight):
    chans = weight.shape[1]
    padded = jnp.pad(vox, ((0, 0), (1, 1), (1, 1), (1, 1), (0, 0)))
    total = jnp.zeros((vox.shape[0] * 64, chans), jnp.float32)
    for dz in range(3):
        for dy in range(3):
            for dx in range(3):
                piece = padded[:, dz : dz + 4, dy : dy + 4, dx : dx + 4].reshape(-1, chans)
                total = total + jnp.dot(
                    piece, weight[(dz * 3 + dy) * 3 + dx], preferred_element_type=jnp.float32
                )
    return total


def select_rows(index, count, values):
    columns = jnp.arange(count, dtype=jnp.int32)
    picker = (index[:, None] == columns[None, :]).astype(jnp.bfloat16)
    return jnp.dot(picker, values, preferred_element_type=jnp.float32).astype(jnp.bfloat16)


def fine_conv(field, table, active, weight):
    bricks = field.shape[0]
    boundary = bricks // 4
    cycle = padded_2(field[:boundary][None, None], (("gz", 0), ("gx", 1)), 1)
    return conv(table, active, weight, field, cycle.reshape(9 * boundary, 3, 16, 128))


def relay_out(buffer, layers, slabs):
    width = buffer.shape[1]
    moved = lax.all_to_all(
        buffer.reshape(layers * slabs, -1, width),
        ("gz", "gx"),
        split_axis=0,
        concat_axis=0,
        tiled=True,
    )
    return moved.reshape(-1, width)


def relay_back(buffer, layers, slabs):
    width = buffer.shape[1]
    moved = lax.all_to_all(
        buffer.reshape(layers * slabs, -1, width),
        ("gz", "gx"),
        split_axis=0,
        concat_axis=0,
        tiled=True,
    )
    return moved.reshape(-1, width)


def on_device(
    features, active_count, neighbors, owner, arrival_cell, w_enc, w_down, w_mid, w_up, w_dec
):
    layers = lax.axis_size("gz")
    slabs = lax.axis_size("gx")
    devices = layers * slabs
    bricks = features.shape[1]
    chans = w_enc.shape[1]
    capacity = arrival_cell.shape[1] // devices
    slot_count = devices * capacity
    blank = jnp.zeros((), jnp.bfloat16)
    live = (jnp.arange(bricks, dtype=jnp.int32) < active_count[0, 0])[:, None]
    x0 = jnp.where(live, features[0], blank)
    zero_index = bricks + 9 * (bricks // 4)
    table = jnp.where(neighbors[0] < 0, zero_index, neighbors[0])
    table = jnp.pad(table, ((0, 1), (0, 0)), constant_values=zero_index).T.reshape(-1)
    active = active_count[0]
    wide = ((0, 0), (0, 0), (0, 128 - chans))
    encoded_dense = fine_conv(dense(x0), table, active, jnp.pad(w_enc, wide))
    encoded = undense(encoded_dense)
    cells = to_cells(encoded.reshape(bricks, 64, chans), chans)
    pooled = jnp.dot(cells.reshape(-1, 8 * chans), w_down, preferred_element_type=jnp.float32)
    pooled = jnp.where(live, pooled.reshape(bricks, 8 * chans), 0.0).astype(jnp.bfloat16)
    target = owner[0]
    later = (
        jnp.arange(bricks, dtype=jnp.int32)[None, :] < jnp.arange(bricks, dtype=jnp.int32)[:, None]
    )
    same = target[:, None] == target[None, :]
    rank = jnp.sum(jnp.logical_and(same, later).astype(jnp.int32), axis=1)
    outgoing_slot = target * capacity + rank
    slot_ids = jnp.arange(slot_count, dtype=jnp.int32)
    scatter_table = (slot_ids[:, None] == outgoing_slot[None, :]).astype(jnp.bfloat16)
    outgoing = jnp.dot(scatter_table, pooled, preferred_element_type=jnp.float32).astype(
        jnp.bfloat16
    )
    incoming = relay_out(outgoing, layers, slabs)
    arrivals = arrival_cell[0]
    cell_ids = jnp.arange(bricks, dtype=jnp.int32)
    landing_table = (cell_ids[:, None] == arrivals[None, :]).astype(jnp.bfloat16)
    coarse = jnp.dot(landing_table, incoming, preferred_element_type=jnp.float32).astype(
        jnp.bfloat16
    )
    coarse_bricks = bricks // 8
    vox = from_cells(coarse.reshape(coarse_bricks, 8, 8 * chans), chans).reshape(
        coarse_bricks, 4, 4, 4, chans
    )
    mixed = coarse_mix(vox, w_mid).reshape(coarse_bricks, 4, 4, 4, chans)
    middle = (vox.astype(jnp.float32) + jax.nn.relu(mixed)).astype(jnp.bfloat16)
    middle_cells = to_cells(middle.reshape(coarse_bricks, 64, chans), chans).reshape(
        bricks, 8 * chans
    )
    reply = select_rows(arrivals, bricks, middle_cells)
    returned = relay_back(reply, layers, slabs)
    back = select_rows(outgoing_slot, slot_count, returned)
    lifted = jnp.dot(back.reshape(bricks * 8, chans), w_up, preferred_element_type=jnp.float32)
    lifted = from_cells(lifted.reshape(bricks, 8, 8 * chans), chans).reshape(bricks, 64 * chans)
    restored = jnp.where(live, encoded.astype(jnp.float32) + lifted, 0.0).astype(jnp.bfloat16)
    decoded = undense(fine_conv(dense(restored), table, active, jnp.pad(w_dec, wide)))
    return decoded[None]


def solution(mesh):
    placed = (
        P("gz", "gx", None),
        P("gz", "gx"),
        P("gz", None, "gx"),
        P("gz", "gx"),
        P("gz", "gx"),
        P(),
        P(),
        P(),
        P(),
        P(),
    )
    return jax.shard_map(
        on_device, mesh=mesh, in_specs=placed, out_specs=P("gz", "gx", None), check_vma=False
    )
```

```python
import functools
import itertools

import jax
import jax.numpy as jnp
from jax import lax
from jax.experimental import pallas as pl
from jax.experimental.pallas import tpu as pltpu
from jax.sharding import PartitionSpec as P

TAPS = 27
ORDER = [[(q - i) % 4 for q in range(4)] for i in range(4)]
CUT = (96, 64, 32)
BLOCK = 32
CHUNKS = ((0, 1), (2, 3), (4, 5), (6,))
MIB = 1024 * 1024
BF16 = jnp.bfloat16
F32 = jnp.float32


def swap_halves(a, b):
    low = lax.broadcasted_iota(jnp.int32, a[0].shape, a[0].ndim - 1) < 64
    turn = lambda x: pltpu.roll(x, 64, x.ndim - 1)
    a1, a2, b0, b1 = turn(a[1]), turn(a[2]), turn(b[0]), turn(b[1])
    first = (a[0], jnp.where(low, a[1], b0), jnp.where(low, b0, b1))
    second = (jnp.where(low, a1, a2), jnp.where(low, a2, b[1]), b[2])
    return first, second


def group_of(cz, sz, cy):
    return ((cz * 2 + sz) * 2 + cy) * 2, sz * 8 + cz * 4 + cy * 2


def to_dense(x):
    rows = [None] * 16
    for cz, sz, cy in itertools.product(range(2), repeat=3):
        g, r = group_of(cz, sz, cy)
        part = lambda s: [x[:, (g + s) * 384 + t * 128 : (g + s) * 384 + (t + 1) * 128] for t in range(3)]
        rows[r], rows[r + 1] = swap_halves(part(0), part(1))
    return [jnp.swapaxes(jnp.stack([row[t] for row in rows], axis=0), 0, 1) for t in range(3)]


def from_dense(tiles):
    rows = [jnp.swapaxes(x, 0, 1) for x in tiles]
    out = [None] * 16
    for cz, sz, cy in itertools.product(range(2), repeat=3):
        g, r = group_of(cz, sz, cy)
        out[g], out[g + 1] = swap_halves([x[r] for x in rows], [x[r + 1] for x in rows])
    return jnp.concatenate([y for x in out for y in x], axis=1)


def dense_kernel(count, x_ref, o_ref):
    first = pl.program_id(0) * 16
    rows = lax.broadcasted_iota(jnp.int32, x_ref.shape, 0) + first
    x = jnp.where(rows < count[0], x_ref[...], jnp.zeros((), BF16))
    for t, y in enumerate(to_dense(x)):
        o_ref[:, t] = y


def make_dense(count, x):
    bricks = x.shape[0]
    return pl.pallas_call(
        dense_kernel,
        grid=(bricks // 16,),
        out_shape=jax.ShapeDtypeStruct((bricks, 3, 16, 128), BF16),
        in_specs=[pl.BlockSpec(memory_space=pltpu.SMEM), pl.BlockSpec((16, x.shape[1]), lambda i: (i, 0))],
        out_specs=pl.BlockSpec((16, 3, 16, 128), lambda i: (i, 0, 0, 0)),
        name="densify",
    )(count, x)


def rotate_range(rot, start, stop):
    wide = lax.broadcasted_iota(jnp.int32, (128, 128), 1)

    def body(m, carry):
        n = pl.multiple_of(m * 8, 8)
        tiles = [rot[0, pl.ds(n, 8), t].reshape(128, 128) for t in range(3)]
        done = []
        for j in range(1, 4):
            amount = (96 * j) % 128
            rolled = [pltpu.roll(x, amount, 1) for x in tiles]
            for u in range(3):
                hi = (128 * u + 127 - 96 * j) // 128 % 3
                lo = (128 * u - 96 * j) // 128 % 3
                done.append((j, u, jnp.where(wide >= amount, rolled[hi], rolled[lo]).reshape(8, 16, 128)))
        for j, u, x in done:
            rot[j, pl.ds(n, 8), u] = x
        return carry

    lax.fori_loop(start // 8, stop // 8, body, 0)


def conv_block(step, table, w_ref, rot):
    lane = lax.broadcasted_iota(jnp.int32, (16, 128), 1)

    def gather(c, b):
        base = (step * BLOCK + b) * 28
        lanes = [[] for _ in range(4)]
        for g in CHUNKS[c]:
            loads = [[rot[j, table[base + 4 * g + j], t] for t in range(3)] for j in range(4)]
            for i in range(4):
                for u in range(3):
                    a, b2 = loads[ORDER[i][u]][u], loads[ORDER[i][u + 1]][u]
                    lanes[i].append(jnp.where(lane < CUT[u], a, b2))
        return lanes

    acc = [None] * 4
    for c in range(len(CHUNKS)):
        got = [gather(c, b) for b in range(BLOCK)]
        for i in range(4):
            lhs = jnp.concatenate([jnp.concatenate(x[i], axis=1) for x in got], axis=0)
            taps = [4 * g + ORDER[i][q] for g in CHUNKS[c] for q in range(4)]
            rhs = jnp.concatenate([w_ref[k] if k < TAPS else jnp.zeros((96, 128), BF16) for k in taps], axis=0)
            part = jnp.dot(lhs, rhs, preferred_element_type=F32)
            acc[i] = part if acc[i] is None else acc[i] + part
    r1 = pltpu.roll(acc[1], 96, 1)
    r2 = pltpu.roll(acc[2], 64, 1)
    r3 = pltpu.roll(acc[3], 32, 1)
    lanes = lax.broadcasted_iota(jnp.int32, acc[0].shape, 1)
    return (jnp.where(lanes < 96, acc[0], r1), jnp.where(lanes < 64, r1, r2), jnp.where(lanes < 32, r2, r3))


def load_field(own, halos, rot, sems):
    bricks = own.shape[0]
    part = halos[0].shape[0]
    total = bricks + len(halos) * part
    copies = [pltpu.make_async_copy(own, rot.at[0, pl.ds(0, bricks)], sems.at[0])]
    for d, piece in enumerate(halos):
        copies.append(pltpu.make_async_copy(piece, rot.at[0, pl.ds(bricks + d * part, part)], sems.at[d + 1]))
    for copy in copies:
        copy.start()
    for j in range(4):
        rot[j, total] = jnp.zeros((3, 16, 128), BF16)
    copies[0].wait()
    rotate_range(rot, 0, bricks)
    for copy in copies[1:]:
        copy.wait()
    rotate_range(rot, bricks, total)


def encode_kernel(table, count, send_slot, w_ref, wd_ref, own, *rest):
    halos, (enc_ref, out_ref, rot, pooled, sems) = rest[:8], rest[8:]
    step = pl.program_id(0)
    bricks = own.shape[0]

    @pl.when(step == 0)
    def _():
        load_field(own, halos, rot, sems)
        pooled[bricks] = jnp.zeros((8, 128), F32)

    tiles = conv_block(step, table, w_ref, rot)
    shape = tiles[0].shape
    live = lax.broadcasted_iota(jnp.int32, shape, 0) // 16 + step * BLOCK < count[0]
    values = []
    for u in range(3):
        mine = rot[0, pl.ds(step * BLOCK, BLOCK), u].reshape(shape).astype(F32)
        value = jnp.where(live, mine + jnp.maximum(tiles[u], 0.0), 0.0).astype(BF16)
        enc_ref[:, u] = value.reshape(BLOCK, 16, 128)
        values.append(value)
    sums = jnp.dot(jnp.concatenate(values, axis=1), wd_ref[...], preferred_element_type=F32)
    sums = sums.reshape(BLOCK, 16, 256)
    sums = sums[:, :8, :128] + sums[:, 8:, 128:]
    pooled[pl.ds(step * BLOCK, BLOCK)] = sums

    @pl.when(step == pl.num_programs(0) - 1)
    def _():
        def place(s, carry):
            out_ref[s] = pooled[send_slot[s]].astype(BF16)
            return carry

        lax.fori_loop(0, out_ref.shape[0], place, 0, unroll=8)


def field_scratch(own, halos):
    total = own.shape[0] + len(halos) * halos[0].shape[0]
    return pltpu.VMEM((4, total + 1, 3, 16, 128), BF16)


SMEM = pl.BlockSpec(memory_space=pltpu.SMEM)
VMEM = pl.BlockSpec(memory_space=pltpu.VMEM)
ANY = pl.BlockSpec(memory_space=pl.ANY)


def encode(table, count, send_slot, w, wd, own, halos):
    bricks = own.shape[0]
    slots = send_slot.shape[0]
    return pl.pallas_call(
        encode_kernel,
        grid=(bricks // BLOCK,),
        out_shape=(
            jax.ShapeDtypeStruct((bricks, 3, 16, 128), BF16),
            jax.ShapeDtypeStruct((slots, 8, 128), BF16),
        ),
        in_specs=[SMEM, SMEM, SMEM, VMEM, VMEM, ANY] + [ANY] * len(halos),
        out_specs=(pl.BlockSpec((BLOCK, 3, 16, 128), lambda i: (i, 0, 0, 0)), VMEM),
        scratch_shapes=[
            field_scratch(own, halos),
            pltpu.VMEM((bricks + 1, 8, 128), F32),
            pltpu.SemaphoreType.DMA((9,)),
        ],
        compiler_params=pltpu.CompilerParams(vmem_limit_bytes=56 * MIB),
        name="encode",
    )(table, count, send_slot, w, wd, own, *halos)


def raw_kernel(table, w_ref, own, *rest):
    halos, (out_ref, rot, sems) = rest[:8], rest[8:]
    step = pl.program_id(0)

    @pl.when(step == 0)
    def _():
        load_field(own, halos, rot, sems)

    for u, tile in enumerate(conv_block(step, table, w_ref, rot)):
        out_ref[:, u] = tile.reshape(BLOCK, 16, 128)


def raw_conv(table, w, own, halos):
    bricks = own.shape[0]
    return pl.pallas_call(
        raw_kernel,
        grid=(bricks // BLOCK,),
        out_shape=jax.ShapeDtypeStruct((bricks, 3, 16, 128), F32),
        in_specs=[SMEM, VMEM, ANY] + [ANY] * len(halos),
        out_specs=pl.BlockSpec((BLOCK, 3, 16, 128), lambda i: (i, 0, 0, 0)),
        scratch_shapes=[field_scratch(own, halos), pltpu.SemaphoreType.DMA((9,))],
        compiler_params=pltpu.CompilerParams(vmem_limit_bytes=56 * MIB),
        cost_estimate=pl.CostEstimate(flops=40_000_000_000, bytes_accessed=13_000_000, transcendentals=0),
        name="raw_conv",
    )(table, w, own, *halos)


def coarse_kernel(from_slot, to_place, w_ref, in_ref, out_ref, cells, grid, turned):
    places = from_slot.shape[0]
    groups = places // 8
    grid[...] = jnp.zeros(grid.shape, BF16)

    def land(p, carry):
        cells[pl.ds(pl.multiple_of(p * 8, 8), 8)] = in_ref[from_slot[p]].astype(F32)
        return carry

    lax.fori_loop(0, places, land, 0, unroll=8)
    voxels = list(itertools.product(range(4), repeat=3))

    def base(z, y, x):
        t = (z // 2) * 4 + (y // 2) * 2 + x // 2
        c = (z % 2) * 4 + (y % 2) * 2 + x % 2
        return t * places + c

    zero = jnp.zeros((32 - groups, 128), F32)
    for z, y, x in voxels:
        piece = cells[pl.ds(base(z, y, x), groups, stride=8)]
        grid[z + 1, y + 1, x + 1] = jnp.concatenate([piece, zero], axis=0).astype(BF16)

    for z in range(4):
        acc = None
        for k0 in range(0, TAPS + 1, 2):
            sides = []
            for k in (k0, min(k0 + 1, TAPS - 1)):
                dz, dy, dx = k // 9, k // 3 % 3, k % 3
                sides.append(grid[z + dz, dy : dy + 4, dx : dx + 4].reshape(16 * 32, 128))
            second = w_ref[k0 + 1] if k0 + 1 < TAPS else jnp.zeros((128, 128), BF16)
            rhs = jnp.concatenate([w_ref[k0], second], axis=0)
            part = jnp.dot(jnp.concatenate(sides, axis=1), rhs, preferred_element_type=F32)
            acc = part if acc is None else acc + part
        acc = acc.reshape(16, 32, 128)
        for y in range(4):
            for x in range(4):
                here = grid[z + 1, y + 1, x + 1].astype(F32) + jnp.maximum(acc[y * 4 + x], 0.0)
                turned[pl.ds(base(z, y, x), groups, stride=8)] = here[:groups]
    turned[pl.ds(places * 8, 8)] = jnp.zeros((8, 128), F32)

    def reply(s, carry):
        out_ref[s] = turned[pl.ds(pl.multiple_of(to_place[s] * 8, 8), 8)].astype(BF16)
        return carry

    lax.fori_loop(0, out_ref.shape[0], reply, 0, unroll=8)


def coarse(from_slot, to_place, w, incoming):
    places = from_slot.shape[0]
    return pl.pallas_call(
        coarse_kernel,
        out_shape=jax.ShapeDtypeStruct(incoming.shape, BF16),
        in_specs=[SMEM, SMEM, VMEM, VMEM],
        out_specs=VMEM,
        scratch_shapes=[
            pltpu.VMEM((places * 8, 128), F32),
            pltpu.VMEM((6, 6, 6, 32, 128), BF16),
            pltpu.VMEM((places * 8 + 8, 128), F32),
        ],
        compiler_params=pltpu.CompilerParams(vmem_limit_bytes=32 * MIB),
        name="coarse_mix",
    )(from_slot, to_place, w, incoming)


def back_kernel(slot, count, in_ref, out_ref):
    def take(b, carry):
        value = in_ref[slot[b]]
        out_ref[b] = jnp.where(b < count[0], value, jnp.zeros_like(value))
        return carry

    lax.fori_loop(0, out_ref.shape[0], take, 0, unroll=8)


def take_back(slot, count, returned):
    return pl.pallas_call(
        back_kernel,
        out_shape=jax.ShapeDtypeStruct((slot.shape[0], 8, 128), BF16),
        in_specs=[SMEM, SMEM, VMEM],
        out_specs=VMEM,
        name="take_back",
    )(slot, count, returned)


def decode_kernel(table, count, w_ref, up_ref, own_ref, raw_ref, enc_ref, *rest):
    halos, (out_ref, cells) = rest[:8], rest[8:]
    step = pl.program_id(0)
    bricks = own_ref.shape[0]
    part = halos[0].shape[0]
    total = bricks + 8 * part

    @pl.when(step == 0)
    def _():
        cells[pl.ds(0, bricks)] = own_ref[...].astype(F32)
        for d, piece in enumerate(halos):
            cells[pl.ds(bricks + d * part, part)] = piece[...].astype(F32)
        cells[total] = jnp.zeros((8, 128), F32)

    block = enc_ref.shape[0]
    acc = None
    for g in range(7):
        columns = []
        for j in range(4):
            rows = [cells[table[(step * block + b) * 28 + 4 * g + j]] for b in range(block)]
            columns.append(jnp.concatenate(rows, axis=0).astype(BF16))
        lhs = jnp.concatenate(columns, axis=1)
        part_sum = jnp.dot(lhs, w_ref[g * 512 : (g + 1) * 512], preferred_element_type=F32)
        acc = part_sum if acc is None else acc + part_sum
    mine = cells[pl.ds(step * block, block)].reshape(block * 8, 128).astype(BF16)
    lifted = jnp.dot(mine, up_ref[...], preferred_element_type=F32)
    live = lax.broadcasted_iota(jnp.int32, (block, 8, 128), 0) + step * block < count[0]
    tiles = []
    for u in range(3):
        halves = []
        coded = enc_ref[:, u].astype(F32)
        for h in range(2):
            lanes = slice(h * 384 + u * 128, h * 384 + (u + 1) * 128)
            restored = coded[:, h * 8 : h * 8 + 8] + lifted[:, lanes].reshape(block, 8, 128)
            restored = restored.astype(BF16).astype(F32)
            mixed = raw_ref[:, u, h * 8 : h * 8 + 8] + acc[:, lanes].reshape(block, 8, 128)
            halves.append(jnp.where(live, restored + jnp.maximum(mixed, 0.0), 0.0))
        tiles.append(jnp.concatenate(halves, axis=1).astype(BF16))
    out_ref[...] = from_dense(tiles)


def decode(table, count, w, up, own, raw, enc, halos):
    bricks = own.shape[0]
    total = bricks + 8 * halos[0].shape[0]
    block = 16
    blocked = lambda: pl.BlockSpec((block, 3, 16, 128), lambda i: (i, 0, 0, 0))
    return pl.pallas_call(
        decode_kernel,
        grid=(bricks // block,),
        out_shape=jax.ShapeDtypeStruct((bricks, 6144), BF16),
        in_specs=[SMEM, SMEM, VMEM, VMEM, VMEM, blocked(), blocked()] + [VMEM] * 8,
        out_specs=pl.BlockSpec((block, 6144), lambda i: (i, 0)),
        scratch_shapes=[pltpu.VMEM((total + 1, 8, 128), F32)],
        compiler_params=pltpu.CompilerParams(vmem_limit_bytes=48 * MIB),
        name="decode",
    )(table, count, w, up, own, raw, enc, *halos)


def halo(face):
    def sides(block, axis):
        count = lax.axis_size(axis)
        forward = [(i, i + 1) for i in range(count - 1)]
        backward = [(target, source) for source, target in forward]
        return lax.ppermute(block, axis, forward), lax.ppermute(block, axis, backward)

    below, above = sides(face, "gz")
    left, right = sides(face, "gx")
    below_left, below_right = sides(below, "gx")
    above_left, above_right = sides(above, "gx")
    return [below_left, below, below_right, left, right, above_left, above, above_right]


def relay(buffer, devices):
    moved = lax.all_to_all(
        buffer.reshape(devices, -1, 128), ("gz", "gx"), split_axis=0, concat_axis=0, tiled=True
    )
    return moved.reshape(-1, 8, 128)


def on_device(
    features, active_count, neighbors, owner, arrival_cell, w_enc, w_down, w_mid, w_up, w_dec
):
    devices = lax.axis_size("gz") * lax.axis_size("gx")
    bricks = features.shape[1]
    boundary = bricks // 4
    chans = w_enc.shape[1]
    spare = 128 - chans
    capacity = arrival_cell.shape[1] // devices
    slot_count = devices * capacity
    count = active_count[0]
    n = neighbors[0]
    m = n - bricks
    side = m // boundary
    n = jnp.where(m >= 4 * boundary, jnp.where(side == 4, m - 4 * boundary, n - boundary), n)
    empty = bricks + 8 * boundary
    table = jnp.pad(jnp.where(n < 0, empty, n), ((0, 1), (0, 0)), constant_values=empty)
    table = table.T.reshape(-1)
    target = owner[0]
    index = jnp.arange(bricks, dtype=jnp.int32)
    same = jnp.logical_and(target[:, None] == target[None, :], index[None, :] < index[:, None])
    slot = target * capacity + jnp.sum(same.astype(jnp.int32), axis=1)
    slot_ids = jnp.arange(slot_count, dtype=jnp.int32)
    send_slot = jnp.min(jnp.where(slot_ids[:, None] == slot[None, :], index[None, :], bricks), axis=1)
    arrivals = arrival_cell[0]
    to_place = jnp.where(arrivals < 0, bricks, arrivals % 8 * (bricks // 8) + arrivals // 8)
    from_slot = jnp.sum(
        jnp.where(index[:, None] == to_place[None, :], slot_ids[None, :], 0), axis=1
    )
    lanes = ((0, 0), (0, 0), (0, spare))
    pooling = jnp.pad(w_down.reshape(2, 4 * chans, chans), lanes)
    pooling = pooling.transpose(1, 0, 2).reshape(4 * chans, 256)
    both = ((0, 0), (0, spare), (0, spare))
    raising = jnp.pad(w_up, ((0, spare), (0, 0)))

    x = make_dense(count, features[0])
    encoded, outgoing = encode(
        table, count, send_slot, jnp.pad(w_enc, lanes), pooling, x, halo(x[:boundary])
    )
    incoming = relay(outgoing, devices)
    encoded_halo = halo(encoded[:boundary])
    reply = coarse(from_slot, to_place, jnp.pad(w_mid, both), incoming)
    returned = relay(reply, devices)
    raw = raw_conv(table, jnp.pad(w_dec, lanes), encoded, encoded_halo)
    lift = jnp.einsum(
        "cse,ked->kcsd", w_up.reshape(chans, 8, chans), w_dec, preferred_element_type=F32
    )
    lift = jnp.pad(lift.astype(BF16).reshape(TAPS, chans, 8 * chans), ((0, 1), (0, spare), (0, 0)))
    lift = lift.reshape(28 * 128, 8 * chans)
    back = take_back(slot, count, returned)
    decoded = decode(
        table, count, lift, raising, back, raw, encoded, halo(back[:boundary])
    )
    return decoded[None]


def solution(mesh):
    placed = (
        P("gz", "gx", None),
        P("gz", "gx"),
        P("gz", None, "gx"),
        P("gz", "gx"),
        P("gz", "gx"),
        P(),
        P(),
        P(),
        P(),
        P(),
    )
    return jax.shard_map(
        on_device, mesh=mesh, in_specs=placed, out_specs=P("gz", "gx", None), check_vma=False
    )
```

```python
import functools
import itertools

import jax
import jax.numpy as jnp
from jax import lax
from jax.experimental import pallas as pl
from jax.experimental.pallas import tpu as pltpu
from jax.sharding import PartitionSpec as P

TAPS = 27
ORDER = [[(q - i) % 4 for q in range(4)] for i in range(4)]
CUT = (96, 64, 32)
BLOCK = 32
CHUNKS = ((0, 1), (2, 3), (4, 5), (6,))
MIB = 1024 * 1024
BF16 = jnp.bfloat16
F32 = jnp.float32


def swap_halves(a, b):
    low = lax.broadcasted_iota(jnp.int32, a[0].shape, a[0].ndim - 1) < 64
    turn = lambda x: pltpu.roll(x, 64, x.ndim - 1)
    a1, a2, b0, b1 = turn(a[1]), turn(a[2]), turn(b[0]), turn(b[1])
    first = (a[0], jnp.where(low, a[1], b0), jnp.where(low, b0, b1))
    second = (jnp.where(low, a1, a2), jnp.where(low, a2, b[1]), b[2])
    return first, second


def group_of(cz, sz, cy):
    return ((cz * 2 + sz) * 2 + cy) * 2, sz * 8 + cz * 4 + cy * 2


def to_dense(x):
    rows = [None] * 16
    for cz, sz, cy in itertools.product(range(2), repeat=3):
        g, r = group_of(cz, sz, cy)
        part = lambda s: [x[:, (g + s) * 384 + t * 128 : (g + s) * 384 + (t + 1) * 128] for t in range(3)]
        rows[r], rows[r + 1] = swap_halves(part(0), part(1))
    return [jnp.swapaxes(jnp.stack([row[t] for row in rows], axis=0), 0, 1) for t in range(3)]


def from_dense(tiles):
    rows = [jnp.swapaxes(x, 0, 1) for x in tiles]
    out = [None] * 16
    for cz, sz, cy in itertools.product(range(2), repeat=3):
        g, r = group_of(cz, sz, cy)
        out[g], out[g + 1] = swap_halves([x[r] for x in rows], [x[r + 1] for x in rows])
    return jnp.concatenate([y for x in out for y in x], axis=1)


OFFSETS = tuple((dz, dx) for dz in (-1, 0, 1) for dx in (-1, 0, 1) if (dz, dx) != (0, 0))
MESH = pl.DeviceIdType.MESH


class Exchange:
    def __init__(self, own, landing, send, recv, chunks):
        self.own, self.landing, self.send, self.recv, self.chunks = own, landing, send, recv, chunks
        self.z, self.x = lax.axis_index("gz"), lax.axis_index("gx")
        self.layers, self.slabs = lax.axis_size("gz"), lax.axis_size("gx")

    def has(self, dz, dx):
        checks = []
        if dz:
            checks.append(self.z > 0 if dz < 0 else self.z < self.layers - 1)
        if dx:
            checks.append(self.x > 0 if dx < 0 else self.x < self.slabs - 1)
        return checks[0] if len(checks) == 1 else jnp.logical_and(*checks)

    def sends(self, slot):
        dz, dx = OFFSETS[slot]
        if dz and dx:
            sides = [self.z > 0 if dz < 0 else self.z < self.layers - 1]
            sides.append(self.x < self.slabs - 1 if dx < 0 else self.x > 0)
            return jnp.logical_and(*sides)
        return self.has(-dz, -dx)

    def copy(self, slot, c):
        dz, dx = OFFSETS[slot]
        if dz and dx:
            source, target = self.landing(OFFSETS.index((dz, 0)), c), (self.z, self.x - dx)
        else:
            source, target = self.own(c), (self.z - dz, self.x - dx)
        return pltpu.make_async_remote_copy(
            src_ref=source,
            dst_ref=self.landing(slot, c),
            send_sem=self.send.at[slot, c],
            recv_sem=self.recv.at[slot, c],
            device_id=target,
            device_id_type=MESH,
        )

    def greet(self):
        barrier = pltpu.get_barrier_semaphore()
        for dz, dx in ((-1, 0), (1, 0), (0, -1), (0, 1)):

            @pl.when(self.has(dz, dx))
            def _():
                pl.semaphore_signal(
                    barrier, inc=1, device_id=(self.z + dz, self.x + dx), device_id_type=MESH
                )

    def meet(self):
        peers = sum(self.has(dz, dx).astype(jnp.int32) for dz, dx in ((-1, 0), (1, 0), (0, -1), (0, 1)))
        pl.semaphore_wait(pltpu.get_barrier_semaphore(), peers)

    def start(self):
        for c in range(self.chunks):
            for slot in (1, 6, 3, 4):

                @pl.when(self.sends(slot))
                def _():
                    self.copy(slot, c).start()

    def forward(self, c):
        for slot, corners in ((1, (0, 2)), (6, (5, 7))):

            @pl.when(self.has(*OFFSETS[slot]))
            def _():
                self.copy(slot, c).wait_recv()

            for corner in corners:

                @pl.when(self.sends(corner))
                def _():
                    self.copy(corner, c).start()

    def arrive(self, slot):
        @pl.when(self.has(*OFFSETS[slot]))
        def _():
            for c in range(self.chunks):
                self.copy(slot, c).wait_recv()

    def finish(self):
        for slot in range(8):

            @pl.when(self.sends(slot))
            def _():
                for c in range(self.chunks):
                    self.copy(slot, c).wait_send()


def rotate_range(rot, start, stop):
    wide = lax.broadcasted_iota(jnp.int32, (128, 128), 1)

    def body(m, carry):
        n = pl.multiple_of(m * 8, 8)
        tiles = [rot[0, pl.ds(n, 8), t].reshape(128, 128) for t in range(3)]
        done = []
        for j in range(1, 4):
            amount = (96 * j) % 128
            rolled = [pltpu.roll(x, amount, 1) for x in tiles]
            for u in range(3):
                hi = (128 * u + 127 - 96 * j) // 128 % 3
                lo = (128 * u - 96 * j) // 128 % 3
                done.append((j, u, jnp.where(wide >= amount, rolled[hi], rolled[lo]).reshape(8, 16, 128)))
        for j, u, x in done:
            rot[j, pl.ds(n, 8), u] = x
        return carry

    lax.fori_loop(start // 8, stop // 8, body, 0)


def conv_block(step, table, w_ref, rot):
    lane = lax.broadcasted_iota(jnp.int32, (16, 128), 1)

    def gather(c, b):
        base = (step * BLOCK + b) * 28
        lanes = [[] for _ in range(4)]
        for g in CHUNKS[c]:
            loads = [[rot[j, table[base + 4 * g + j], t] for t in range(3)] for j in range(4)]
            for i in range(4):
                for u in range(3):
                    a, b2 = loads[ORDER[i][u]][u], loads[ORDER[i][u + 1]][u]
                    lanes[i].append(jnp.where(lane < CUT[u], a, b2))
        return lanes

    acc = [None] * 4
    for c in range(len(CHUNKS)):
        got = [gather(c, b) for b in range(BLOCK)]
        for i in range(4):
            lhs = jnp.concatenate([jnp.concatenate(x[i], axis=1) for x in got], axis=0)
            taps = [4 * g + ORDER[i][q] for g in CHUNKS[c] for q in range(4)]
            rhs = jnp.concatenate([w_ref[k] if k < TAPS else jnp.zeros((96, 128), BF16) for k in taps], axis=0)
            part = jnp.dot(lhs, rhs, preferred_element_type=F32)
            acc[i] = part if acc[i] is None else acc[i] + part
    r1 = pltpu.roll(acc[1], 96, 1)
    r2 = pltpu.roll(acc[2], 64, 1)
    r3 = pltpu.roll(acc[3], 32, 1)
    lanes = lax.broadcasted_iota(jnp.int32, acc[0].shape, 1)
    return (jnp.where(lanes < 96, acc[0], r1), jnp.where(lanes < 64, r1, r2), jnp.where(lanes < 32, r2, r3))


def encode_kernel(
    parts, table, count, send_slot, w_ref, wd_ref, x_ref,
    enc_ref, out_ref, halo_ref, rot, pooled, face, sends, recvs, sends2, recvs2,
):
    step = pl.program_id(0)
    bricks = x_ref.shape[0]
    part = bricks // 4
    size = part // parts
    total = bricks + 8 * part
    first = Exchange(
        lambda c: rot.at[0, pl.ds(c * size, size)],
        lambda slot, c: rot.at[0, pl.ds(bricks + slot * part + c * size, size)],
        sends, recvs, parts,
    )
    second = Exchange(
        lambda c: face.at[pl.ds(c * size, size)],
        lambda slot, c: halo_ref.at[slot, pl.ds(c * size, size)],
        sends2, recvs2, parts,
    )

    def fill(slot):
        begin = bricks + slot * part
        first.arrive(slot) if OFFSETS[slot][1] else None

        @pl.when(jnp.logical_not(first.has(*OFFSETS[slot])))
        def _():
            def clear(n, carry):
                rot[0, begin + n] = jnp.zeros((3, 16, 128), BF16)
                return carry

            lax.fori_loop(0, part, clear, 0)

        rotate_range(rot, begin, begin + part)

    def densify(start, stop):
        def body(m, carry):
            begin = pl.multiple_of(m * 16, 16)
            x = x_ref[pl.ds(begin, 16)]
            live = lax.broadcasted_iota(jnp.int32, x.shape, 0) + begin < count[0]
            for t, y in enumerate(to_dense(jnp.where(live, x, jnp.zeros((), BF16)))):
                rot[0, pl.ds(begin, 16), t] = y
            return carry

        lax.fori_loop(start // 16, stop // 16, body, 0)

    @pl.when(step == 0)
    def _():
        first.greet()
        densify(0, part)
        first.meet()
        first.start()
        for j in range(4):
            rot[j, total] = jnp.zeros((3, 16, 128), BF16)
        pooled[bricks] = jnp.zeros((8, 128), F32)
        densify(part, bricks)
        first.forward(0)
        rotate_range(rot, 0, bricks)
        first.forward(1)
        fill(3)
        fill(4)
        first.forward(2)
        for slot in (1, 6, 0, 2, 5, 7):
            fill(slot)
        first.finish()

    tiles = conv_block(step, table, w_ref, rot)
    shape = tiles[0].shape
    live = lax.broadcasted_iota(jnp.int32, shape, 0) // 16 + step * BLOCK < count[0]
    values = []
    for u in range(3):
        mine = rot[0, pl.ds(step * BLOCK, BLOCK), u].reshape(shape).astype(F32)
        value = jnp.where(live, mine + jnp.maximum(tiles[u], 0.0), 0.0).astype(BF16)
        enc_ref[:, u] = value.reshape(BLOCK, 16, 128)
        values.append(value)
    sums = jnp.dot(jnp.concatenate(values, axis=1), wd_ref[...], preferred_element_type=F32)
    sums = sums.reshape(BLOCK, 16, 256)
    sums = sums[:, :8, :128] + sums[:, 8:, 128:]
    pooled[pl.ds(step * BLOCK, BLOCK)] = sums

    @pl.when(step == 0)
    def _():
        face[pl.ds(0, BLOCK)] = enc_ref[...]

    @pl.when(step == 1)
    def _():
        face[pl.ds(BLOCK, part - BLOCK)] = enc_ref[: part - BLOCK]
        second.start()

    for c in range(parts):

        @pl.when(step == c + 2)
        def _():
            second.forward(c)

    @pl.when(step == pl.num_programs(0) - 1)
    def _():
        def place(s, carry):
            out_ref[s] = pooled[send_slot[s]].astype(BF16)
            return carry

        lax.fori_loop(0, out_ref.shape[0], place, 0, unroll=8)
        for slot in (0, 2, 3, 4, 5, 7):
            second.arrive(slot)
        second.finish()


def field_scratch(own, halos):
    total = own.shape[0] + len(halos) * halos[0].shape[0]
    return pltpu.VMEM((4, total + 1, 3, 16, 128), BF16)


SMEM = pl.BlockSpec(memory_space=pltpu.SMEM)
VMEM = pl.BlockSpec(memory_space=pltpu.VMEM)
ANY = pl.BlockSpec(memory_space=pl.ANY)


def encode(table, count, send_slot, w, wd, x):
    bricks = x.shape[0]
    part = bricks // 4
    slots = send_slot.shape[0]
    parts = 3
    sems = pltpu.SemaphoreType.DMA((8, parts))
    return pl.pallas_call(
        functools.partial(encode_kernel, parts),
        grid=(bricks // BLOCK,),
        out_shape=(
            jax.ShapeDtypeStruct((bricks, 3, 16, 128), BF16),
            jax.ShapeDtypeStruct((slots, 8, 128), BF16),
            jax.ShapeDtypeStruct((8, part, 3, 16, 128), BF16),
        ),
        in_specs=[SMEM, SMEM, SMEM, VMEM, VMEM, VMEM],
        out_specs=(pl.BlockSpec((BLOCK, 3, 16, 128), lambda i: (i, 0, 0, 0)), VMEM, ANY),
        scratch_shapes=[
            pltpu.VMEM((4, bricks + 8 * part + 1, 3, 16, 128), BF16),
            pltpu.VMEM((bricks + 1, 8, 128), F32),
            pltpu.VMEM((part, 3, 16, 128), BF16),
            sems, sems, sems, sems,
        ],
        compiler_params=pltpu.CompilerParams(
            vmem_limit_bytes=56 * MIB, collective_id=1, has_side_effects=True
        ),
        name="encode",
    )(table, count, send_slot, w, wd, x)


def raw_kernel(table, w_ref, own, halo_ref, out_ref, rot, sems):
    step = pl.program_id(0)
    bricks = own.shape[0]
    part = halo_ref.shape[1]
    total = bricks + 8 * part
    side = Exchange(None, None, None, None, 1)

    @pl.when(step == 0)
    def _():
        mine = pltpu.make_async_copy(own, rot.at[0, pl.ds(0, bricks)], sems.at[8])
        mine.start()
        piece = lambda slot: pltpu.make_async_copy(
            halo_ref.at[slot], rot.at[0, pl.ds(bricks + slot * part, part)], sems.at[slot]
        )
        for slot in range(8):

            @pl.when(side.has(*OFFSETS[slot]))
            def _():
                piece(slot).start()

        for j in range(4):
            rot[j, total] = jnp.zeros((3, 16, 128), BF16)
        mine.wait()
        rotate_range(rot, 0, bricks)
        for slot in range(8):
            here = side.has(*OFFSETS[slot])

            @pl.when(here)
            def _():
                piece(slot).wait()

            @pl.when(jnp.logical_not(here))
            def _():
                def clear(n, carry):
                    rot[0, bricks + slot * part + n] = jnp.zeros((3, 16, 128), BF16)
                    return carry

                lax.fori_loop(0, part, clear, 0)

        rotate_range(rot, bricks, total)

    for u, tile in enumerate(conv_block(step, table, w_ref, rot)):
        out_ref[:, u] = tile.reshape(BLOCK, 16, 128)


def raw_conv(table, w, own, halos):
    bricks = own.shape[0]
    total = bricks + 8 * halos.shape[1]
    return pl.pallas_call(
        raw_kernel,
        grid=(bricks // BLOCK,),
        out_shape=jax.ShapeDtypeStruct((bricks, 3, 16, 128), F32),
        in_specs=[SMEM, VMEM, ANY, ANY],
        out_specs=pl.BlockSpec((BLOCK, 3, 16, 128), lambda i: (i, 0, 0, 0)),
        scratch_shapes=[pltpu.VMEM((4, total + 1, 3, 16, 128), BF16), pltpu.SemaphoreType.DMA((9,))],
        compiler_params=pltpu.CompilerParams(vmem_limit_bytes=56 * MIB),
        cost_estimate=pl.CostEstimate(flops=40_000_000_000, bytes_accessed=13_000_000, transcendentals=0),
        name="raw_conv",
    )(table, w, own, halos)


def coarse_kernel(from_slot, to_place, w_ref, in_ref, out_ref, cells, grid, turned):
    places = from_slot.shape[0]
    groups = places // 8
    grid[...] = jnp.zeros(grid.shape, BF16)

    def land(p, carry):
        cells[pl.ds(pl.multiple_of(p * 8, 8), 8)] = in_ref[from_slot[p]].astype(F32)
        return carry

    lax.fori_loop(0, places, land, 0, unroll=8)
    voxels = list(itertools.product(range(4), repeat=3))

    def base(z, y, x):
        t = (z // 2) * 4 + (y // 2) * 2 + x // 2
        c = (z % 2) * 4 + (y % 2) * 2 + x % 2
        return t * places + c

    zero = jnp.zeros((32 - groups, 128), F32)
    for z, y, x in voxels:
        piece = cells[pl.ds(base(z, y, x), groups, stride=8)]
        grid[z + 1, y + 1, x + 1] = jnp.concatenate([piece, zero], axis=0).astype(BF16)

    for z in range(4):
        acc = None
        for k0 in range(0, TAPS + 1, 2):
            sides = []
            for k in (k0, min(k0 + 1, TAPS - 1)):
                dz, dy, dx = k // 9, k // 3 % 3, k % 3
                sides.append(grid[z + dz, dy : dy + 4, dx : dx + 4].reshape(16 * 32, 128))
            second = w_ref[k0 + 1] if k0 + 1 < TAPS else jnp.zeros((128, 128), BF16)
            rhs = jnp.concatenate([w_ref[k0], second], axis=0)
            part = jnp.dot(jnp.concatenate(sides, axis=1), rhs, preferred_element_type=F32)
            acc = part if acc is None else acc + part
        acc = acc.reshape(16, 32, 128)
        for y in range(4):
            for x in range(4):
                here = grid[z + 1, y + 1, x + 1].astype(F32) + jnp.maximum(acc[y * 4 + x], 0.0)
                turned[pl.ds(base(z, y, x), groups, stride=8)] = here[:groups]
    turned[pl.ds(places * 8, 8)] = jnp.zeros((8, 128), F32)

    def reply(s, carry):
        out_ref[s] = turned[pl.ds(pl.multiple_of(to_place[s] * 8, 8), 8)].astype(BF16)
        return carry

    lax.fori_loop(0, out_ref.shape[0], reply, 0, unroll=8)


def coarse(from_slot, to_place, w, incoming):
    places = from_slot.shape[0]
    return pl.pallas_call(
        coarse_kernel,
        out_shape=jax.ShapeDtypeStruct(incoming.shape, BF16),
        in_specs=[SMEM, SMEM, VMEM, VMEM],
        out_specs=VMEM,
        scratch_shapes=[
            pltpu.VMEM((places * 8, 128), F32),
            pltpu.VMEM((6, 6, 6, 32, 128), BF16),
            pltpu.VMEM((places * 8 + 8, 128), F32),
        ],
        compiler_params=pltpu.CompilerParams(vmem_limit_bytes=32 * MIB),
        name="coarse_mix",
    )(from_slot, to_place, w, incoming)


def spread_kernel(slot, count, in_ref, out_ref, face, landed, sends, recvs):
    bricks = slot.shape[0]
    part = bricks // 4
    ring = Exchange(lambda c: face, lambda k, c: landed.at[k], sends, recvs, 1)
    ring.greet()

    def take(b, carry):
        value = in_ref[slot[b]].astype(F32)
        out_ref[b] = jnp.where(b < count[0], value, 0.0)
        return carry

    lax.fori_loop(0, part, take, 0, unroll=8)
    face[...] = out_ref[pl.ds(0, part)].reshape(face.shape).astype(BF16)
    ring.meet()
    ring.start()
    lax.fori_loop(part, bricks, take, 0, unroll=8)
    out_ref[bricks + 8 * part] = jnp.zeros((8, 128), F32)
    ring.forward(0)
    for k in (3, 4, 1, 6, 0, 2, 5, 7):
        begin = bricks + k * part
        here = ring.has(*OFFSETS[k])
        if OFFSETS[k][1]:
            ring.arrive(k)

        @pl.when(here)
        def _():
            out_ref[pl.ds(begin, part)] = landed[k].astype(F32).reshape(part, 8, 128)

        @pl.when(jnp.logical_not(here))
        def _():
            out_ref[pl.ds(begin, part)] = jnp.zeros((part, 8, 128), F32)

    ring.finish()


def spread(slot, count, returned):
    bricks = slot.shape[0]
    part = bricks // 4
    return pl.pallas_call(
        spread_kernel,
        out_shape=jax.ShapeDtypeStruct((bricks + 8 * part + 1, 8, 128), F32),
        in_specs=[SMEM, SMEM, VMEM],
        out_specs=VMEM,
        scratch_shapes=[
            pltpu.VMEM((part // 2, 16, 128), BF16),
            pltpu.VMEM((8, part // 2, 16, 128), BF16),
            pltpu.SemaphoreType.DMA((8, 1)),
            pltpu.SemaphoreType.DMA((8, 1)),
        ],
        compiler_params=pltpu.CompilerParams(
            vmem_limit_bytes=16 * MIB, collective_id=2, has_side_effects=True
        ),
        name="spread",
    )(slot, count, returned)


def decode_kernel(table, count, w_ref, up_ref, cells, raw_ref, enc_ref, out_ref):
    step = pl.program_id(0)
    block = enc_ref.shape[0]
    acc = None
    for g in range(7):
        columns = []
        for j in range(4):
            rows = [cells[table[(step * block + b) * 28 + 4 * g + j]] for b in range(block)]
            columns.append(jnp.concatenate(rows, axis=0).astype(BF16))
        lhs = jnp.concatenate(columns, axis=1)
        part_sum = jnp.dot(lhs, w_ref[g * 512 : (g + 1) * 512], preferred_element_type=F32)
        acc = part_sum if acc is None else acc + part_sum
    mine = cells[pl.ds(step * block, block)].reshape(block * 8, 128).astype(BF16)
    lifted = jnp.dot(mine, up_ref[...], preferred_element_type=F32)
    live = lax.broadcasted_iota(jnp.int32, (block, 8, 128), 0) + step * block < count[0]
    tiles = []
    for u in range(3):
        halves = []
        coded = enc_ref[:, u].astype(F32)
        for h in range(2):
            lanes = slice(h * 384 + u * 128, h * 384 + (u + 1) * 128)
            restored = coded[:, h * 8 : h * 8 + 8] + lifted[:, lanes].reshape(block, 8, 128)
            restored = restored.astype(BF16).astype(F32)
            mixed = raw_ref[:, u, h * 8 : h * 8 + 8] + acc[:, lanes].reshape(block, 8, 128)
            halves.append(jnp.where(live, restored + jnp.maximum(mixed, 0.0), 0.0))
        tiles.append(jnp.concatenate(halves, axis=1).astype(BF16))
    for b in range(0, block, 16):
        out_ref[b : b + 16] = from_dense([x[b : b + 16] for x in tiles])


def decode(table, count, w, up, cells, raw, enc, block=48):
    bricks = enc.shape[0]
    blocked = lambda: pl.BlockSpec((block, 3, 16, 128), lambda i: (i, 0, 0, 0))
    return pl.pallas_call(
        decode_kernel,
        grid=(bricks // block,),
        out_shape=jax.ShapeDtypeStruct((bricks, 6144), BF16),
        in_specs=[SMEM, SMEM, VMEM, VMEM, VMEM, blocked(), blocked()],
        out_specs=pl.BlockSpec((block, 6144), lambda i: (i, 0)),
        compiler_params=pltpu.CompilerParams(vmem_limit_bytes=48 * MIB),
        name="decode",
    )(table, count, w, up, cells, raw, enc)


def relay(buffer, devices):
    moved = lax.all_to_all(
        buffer.reshape(devices, -1, 128), ("gz", "gx"), split_axis=0, concat_axis=0, tiled=True
    )
    return moved.reshape(-1, 8, 128)


def on_device(
    features, active_count, neighbors, owner, arrival_cell, w_enc, w_down, w_mid, w_up, w_dec
):
    devices = lax.axis_size("gz") * lax.axis_size("gx")
    bricks = features.shape[1]
    boundary = bricks // 4
    chans = w_enc.shape[1]
    spare = 128 - chans
    capacity = arrival_cell.shape[1] // devices
    slot_count = devices * capacity
    count = active_count[0]
    n = neighbors[0]
    m = n - bricks
    side = m // boundary
    n = jnp.where(m >= 4 * boundary, jnp.where(side == 4, m - 4 * boundary, n - boundary), n)
    empty = bricks + 8 * boundary
    table = jnp.pad(jnp.where(n < 0, empty, n), ((0, 1), (0, 0)), constant_values=empty)
    table = table.T.reshape(-1)
    target = owner[0]
    index = jnp.arange(bricks, dtype=jnp.int32)
    same = jnp.logical_and(target[:, None] == target[None, :], index[None, :] < index[:, None])
    slot = target * capacity + jnp.sum(same.astype(jnp.int32), axis=1)
    slot_ids = jnp.arange(slot_count, dtype=jnp.int32)
    send_slot = jnp.min(jnp.where(slot_ids[:, None] == slot[None, :], index[None, :], bricks), axis=1)
    arrivals = arrival_cell[0]
    to_place = jnp.where(arrivals < 0, bricks, arrivals % 8 * (bricks // 8) + arrivals // 8)
    from_slot = jnp.sum(
        jnp.where(index[:, None] == to_place[None, :], slot_ids[None, :], 0), axis=1
    )
    lanes = ((0, 0), (0, 0), (0, spare))
    pooling = jnp.pad(w_down.reshape(2, 4 * chans, chans), lanes)
    pooling = pooling.transpose(1, 0, 2).reshape(4 * chans, 256)
    both = ((0, 0), (0, spare), (0, spare))
    raising = jnp.pad(w_up, ((0, spare), (0, 0)))

    encoded, outgoing, encoded_halo = encode(
        table, count, send_slot, jnp.pad(w_enc, lanes), pooling, features[0]
    )
    incoming = relay(outgoing, devices)
    reply = coarse(from_slot, to_place, jnp.pad(w_mid, both), incoming)
    returned = relay(reply, devices)
    raw = raw_conv(table, jnp.pad(w_dec, lanes), encoded, encoded_halo)
    lift = jnp.einsum(
        "cse,ked->kcsd", w_up.reshape(chans, 8, chans), w_dec, preferred_element_type=F32
    )
    lift = jnp.pad(lift.astype(BF16).reshape(TAPS, chans, 8 * chans), ((0, 1), (0, spare), (0, 0)))
    lift = lift.reshape(28 * 128, 8 * chans)
    cells = spread(slot, count, returned)
    decoded = decode(table, count, lift, raising, cells, raw, encoded)
    return decoded[None]


def solution(mesh):
    placed = (
        P("gz", "gx", None),
        P("gz", "gx"),
        P("gz", None, "gx"),
        P("gz", "gx"),
        P("gz", "gx"),
        P(),
        P(),
        P(),
        P(),
        P(),
    )
    return jax.shard_map(
        on_device, mesh=mesh, in_specs=placed, out_specs=P("gz", "gx", None), check_vma=False
    )
```

```python
import functools
import itertools

import jax
import jax.numpy as jnp
from jax import lax
from jax.experimental import pallas as pl
from jax.experimental.pallas import tpu as pltpu
from jax.sharding import PartitionSpec as P

TAPS = 27
ORDER = [[(q - i) % 4 for q in range(4)] for i in range(4)]
CUT = (96, 64, 32)
BLOCK = 32
CHUNKS = ((0, 1), (2, 3), (4, 5), (6,))
MIB = 1024 * 1024
BF16 = jnp.bfloat16
F32 = jnp.float32


def swap_halves(a, b):
    low = lax.broadcasted_iota(jnp.int32, a[0].shape, a[0].ndim - 1) < 64
    turn = lambda x: pltpu.roll(x, 64, x.ndim - 1)
    a1, a2, b0, b1 = turn(a[1]), turn(a[2]), turn(b[0]), turn(b[1])
    first = (a[0], jnp.where(low, a[1], b0), jnp.where(low, b0, b1))
    second = (jnp.where(low, a1, a2), jnp.where(low, a2, b[1]), b[2])
    return first, second


def group_of(cz, sz, cy):
    return ((cz * 2 + sz) * 2 + cy) * 2, sz * 8 + cz * 4 + cy * 2


def to_dense(x):
    rows = [None] * 16
    for cz, sz, cy in itertools.product(range(2), repeat=3):
        g, r = group_of(cz, sz, cy)
        part = lambda s: [x[:, (g + s) * 384 + t * 128 : (g + s) * 384 + (t + 1) * 128] for t in range(3)]
        rows[r], rows[r + 1] = swap_halves(part(0), part(1))
    return [jnp.swapaxes(jnp.stack([row[t] for row in rows], axis=0), 0, 1) for t in range(3)]


def from_dense(tiles):
    rows = [jnp.swapaxes(x, 0, 1) for x in tiles]
    out = [None] * 16
    for cz, sz, cy in itertools.product(range(2), repeat=3):
        g, r = group_of(cz, sz, cy)
        out[g], out[g + 1] = swap_halves([x[r] for x in rows], [x[r + 1] for x in rows])
    return jnp.concatenate([y for x in out for y in x], axis=1)


OFFSETS = tuple((dz, dx) for dz in (-1, 0, 1) for dx in (-1, 0, 1) if (dz, dx) != (0, 0))
MESH = pl.DeviceIdType.MESH


class Exchange:
    def __init__(self, own, landing, send, recv, chunks):
        self.own, self.landing, self.send, self.recv, self.chunks = own, landing, send, recv, chunks
        self.z, self.x = lax.axis_index("gz"), lax.axis_index("gx")
        self.layers, self.slabs = lax.axis_size("gz"), lax.axis_size("gx")

    def has(self, dz, dx):
        checks = []
        if dz:
            checks.append(self.z > 0 if dz < 0 else self.z < self.layers - 1)
        if dx:
            checks.append(self.x > 0 if dx < 0 else self.x < self.slabs - 1)
        return checks[0] if len(checks) == 1 else jnp.logical_and(*checks)

    def sends(self, slot):
        dz, dx = OFFSETS[slot]
        if dz and dx:
            sides = [self.z > 0 if dz < 0 else self.z < self.layers - 1]
            sides.append(self.x < self.slabs - 1 if dx < 0 else self.x > 0)
            return jnp.logical_and(*sides)
        return self.has(-dz, -dx)

    def copy(self, slot, c):
        dz, dx = OFFSETS[slot]
        if dz and dx:
            source, target = self.landing(OFFSETS.index((dz, 0)), c), (self.z, self.x - dx)
        else:
            source, target = self.own(c), (self.z - dz, self.x - dx)
        return pltpu.make_async_remote_copy(
            src_ref=source,
            dst_ref=self.landing(slot, c),
            send_sem=self.send.at[slot, c],
            recv_sem=self.recv.at[slot, c],
            device_id=target,
            device_id_type=MESH,
        )

    def greet(self):
        barrier = pltpu.get_barrier_semaphore()
        for dz, dx in ((-1, 0), (1, 0), (0, -1), (0, 1)):

            @pl.when(self.has(dz, dx))
            def _():
                pl.semaphore_signal(
                    barrier, inc=1, device_id=(self.z + dz, self.x + dx), device_id_type=MESH
                )

    def meet(self):
        peers = sum(self.has(dz, dx).astype(jnp.int32) for dz, dx in ((-1, 0), (1, 0), (0, -1), (0, 1)))
        pl.semaphore_wait(pltpu.get_barrier_semaphore(), peers)

    def start(self, *chunks):
        for c in chunks:
            for slot in (1, 6, 3, 4):

                @pl.when(self.sends(slot))
                def _():
                    self.copy(slot, c).start()

    def forward(self, c):
        for slot, corners in ((1, (0, 2)), (6, (5, 7))):

            @pl.when(self.has(*OFFSETS[slot]))
            def _():
                self.copy(slot, c).wait_recv()

            for corner in corners:

                @pl.when(self.sends(corner))
                def _():
                    self.copy(corner, c).start()

    def arrive(self, slot):
        @pl.when(self.has(*OFFSETS[slot]))
        def _():
            for c in range(self.chunks):
                self.copy(slot, c).wait_recv()

    def finish(self):
        for slot in range(8):

            @pl.when(self.sends(slot))
            def _():
                for c in range(self.chunks):
                    self.copy(slot, c).wait_send()


def rotate_range(rot, start, stop, size=48):
    rows = size * 16
    wide = lax.broadcasted_iota(jnp.int32, (rows, 128), 1)
    source = lax.broadcasted_iota(jnp.int32, (128, 384), 0)
    lane = lax.broadcasted_iota(jnp.int32, (128, 384), 1)
    shift = jnp.where(lane < 128, 96, jnp.where(lane < 256, 64, 32))
    turn = (source == ((lane - shift) & 127)).astype(F32).astype(BF16)

    def body(m, carry):
        n = pl.multiple_of(start + m * size, 16)
        tiles = [rot[0, pl.ds(n, size), t].reshape(rows, 128) for t in range(3)]
        turned = jnp.dot(tiles[0], turn, preferred_element_type=F32).astype(BF16)
        done = []
        for j in range(1, 4):
            amount = (96 * j) % 128
            rolled = [turned[:, (j - 1) * 128 : j * 128]]
            rolled += [pltpu.roll(x, amount, 1) for x in tiles[1:]]
            for u in range(3):
                hi = (128 * u + 127 - 96 * j) // 128 % 3
                lo = (128 * u - 96 * j) // 128 % 3
                done.append((j, u, jnp.where(wide >= amount, rolled[hi], rolled[lo]).reshape(size, 16, 128)))
        for j, u, x in done:
            rot[j, pl.ds(n, size), u] = x
        return carry

    lax.fori_loop(0, (stop - start) // size, body, 0)


def widen(wide, w_ref):
    wide[...] = jnp.zeros(wide.shape, BF16)
    for k in range(w_ref.shape[0]):
        wide[k, : w_ref.shape[1], : w_ref.shape[2]] = w_ref[k]


def conv_block(step, table, w_ref, rot):
    lane = lax.broadcasted_iota(jnp.int32, (16, 128), 1)

    def gather(c, b):
        brick = step * BLOCK + b
        lanes = [[] for _ in range(4)]
        for g in CHUNKS[c]:
            loads = []
            for j in range(4):
                if 4 * g + j < TAPS:
                    n = table[4 * g + j, brick]
                    loads.append([rot[j, n, t] for t in range(3)])
                else:
                    loads.append([jnp.zeros((16, 128), BF16)] * 3)
            for i in range(4):
                for u in range(3):
                    a, b2 = loads[ORDER[i][u]][u], loads[ORDER[i][u + 1]][u]
                    lanes[i].append(jnp.where(lane < CUT[u], a, b2))
        return lanes

    acc = [None] * 4
    for c in range(len(CHUNKS)):
        got = [gather(c, b) for b in range(BLOCK)]
        for i in range(4):
            lhs = jnp.concatenate([jnp.concatenate(x[i], axis=1) for x in got], axis=0)
            taps = [4 * g + ORDER[i][q] for g in CHUNKS[c] for q in range(4)]
            rhs = jnp.concatenate([w_ref[k] for k in taps], axis=0)
            part = jnp.dot(lhs, rhs, preferred_element_type=F32)
            acc[i] = part if acc[i] is None else acc[i] + part
    r1 = pltpu.roll(acc[1], 96, 1)
    r2 = pltpu.roll(acc[2], 64, 1)
    r3 = pltpu.roll(acc[3], 32, 1)
    lanes = lax.broadcasted_iota(jnp.int32, acc[0].shape, 1)
    return (jnp.where(lanes < 96, acc[0], r1), jnp.where(lanes < 64, r1, r2), jnp.where(lanes < 32, r2, r3))


def encode_kernel(
    parts, parts2, table, count, send_slot, w_in, wd_in, x_ref,
    enc_ref, out_ref, halo_ref, rot, pooled, face, w_ref, wd_ref, sends, recvs, sends2, recvs2,
):
    step = pl.program_id(0)
    bricks = x_ref.shape[0]
    part = bricks // 4
    size = part // parts
    size2 = part // parts2
    total = bricks + 8 * part
    first = Exchange(
        lambda c: rot.at[0, pl.ds(c * size, size)],
        lambda slot, c: rot.at[0, pl.ds(bricks + slot * part + c * size, size)],
        sends, recvs, parts,
    )
    second = Exchange(
        lambda c: face.at[pl.ds(c * size2, size2)],
        lambda slot, c: halo_ref.at[slot, pl.ds(c * size2, size2)],
        sends2, recvs2, parts2,
    )

    def fill(slot):
        begin = bricks + slot * part
        first.arrive(slot) if OFFSETS[slot][1] else None

        @pl.when(jnp.logical_not(first.has(*OFFSETS[slot])))
        def _():
            def clear(n, carry):
                rot[0, begin + n] = jnp.zeros((3, 16, 128), BF16)
                return carry

            lax.fori_loop(0, part, clear, 0)

        rotate_range(rot, begin, begin + part)

    def densify(start, stop):
        def body(m, carry):
            begin = pl.multiple_of(m * 16, 16)
            x = x_ref[pl.ds(begin, 16)]
            live = lax.broadcasted_iota(jnp.int32, x.shape, 0) + begin < count[0]
            for t, y in enumerate(to_dense(jnp.where(live, x, jnp.zeros((), BF16)))):
                rot[0, pl.ds(begin, 16), t] = y
            return carry

        lax.fori_loop(start // 16, stop // 16, body, 0)

    @pl.when(step == 0)
    def _():
        first.greet()
        densify(0, part)
        first.meet()
        first.start(*range(parts))
        for j in range(4):
            rot[j, total] = jnp.zeros((3, 16, 128), BF16)
        pooled[bricks] = jnp.zeros((8, 128), F32)
        widen(w_ref, w_in)
        wd_ref[...] = jnp.zeros(wd_ref.shape, BF16)
        half, chans = wd_in.shape[0] // 2, wd_in.shape[1]
        wd_ref[:, :chans] = wd_in[:half]
        wd_ref[:, 128 : 128 + chans] = wd_in[half:]
        densify(part, 2 * part)
        first.forward(0)
        densify(2 * part, 3 * part)
        first.forward(1)
        densify(3 * part, bricks)
        first.forward(2)
        rotate_range(rot, 0, 2 * part)
        first.forward(3)
        rotate_range(rot, 2 * part, bricks)
        first.forward(4)
        fill(3)
        fill(4)
        first.forward(5)
        for slot in (1, 6, 0, 2, 5, 7):
            fill(slot)
        first.finish()

    tiles = conv_block(step, table, w_ref, rot)
    shape = tiles[0].shape
    live = lax.broadcasted_iota(jnp.int32, shape, 0) // 16 + step * BLOCK < count[0]
    values = []
    for u in range(3):
        mine = rot[0, pl.ds(step * BLOCK, BLOCK), u].reshape(shape).astype(F32)
        value = jnp.where(live, mine + jnp.maximum(tiles[u], 0.0), 0.0).astype(BF16)
        enc_ref[:, u] = value.reshape(BLOCK, 16, 128)
        values.append(value)
    sums = jnp.dot(jnp.concatenate(values, axis=1), wd_ref[...], preferred_element_type=F32)
    sums = sums.reshape(BLOCK, 16, 256)
    sums = sums[:, :8, :128] + sums[:, 8:, 128:]
    pooled[pl.ds(step * BLOCK, BLOCK)] = sums

    @pl.when(step == 0)
    def _():
        face[pl.ds(0, BLOCK)] = enc_ref[...]
        second.start(0, 1)

    @pl.when(step == 1)
    def _():
        face[pl.ds(BLOCK, part - BLOCK)] = enc_ref[: part - BLOCK]
        second.start(2)

    @pl.when(step == 2)
    def _():
        second.forward(0)

    @pl.when(step == 3)
    def _():
        second.forward(1)
        second.forward(2)

    @pl.when(step == pl.num_programs(0) - 1)
    def _():
        def place(s, carry):
            out_ref[s] = pooled[send_slot[s]].astype(BF16)
            return carry

        lax.fori_loop(0, out_ref.shape[0], place, 0, unroll=8)
        for slot in (0, 2, 3, 4, 5, 7):
            second.arrive(slot)
        second.finish()


def field_scratch(own, halos):
    total = own.shape[0] + len(halos) * halos[0].shape[0]
    return pltpu.VMEM((4, total + 1, 3, 16, 128), BF16)


SMEM = pl.BlockSpec(memory_space=pltpu.SMEM)
VMEM = pl.BlockSpec(memory_space=pltpu.VMEM)
ANY = pl.BlockSpec(memory_space=pl.ANY)


def encode(table, count, send_slot, w, wd, x):
    bricks = x.shape[0]
    part = bricks // 4
    slots = send_slot.shape[0]
    parts, parts2 = 6, 3
    sems = pltpu.SemaphoreType.DMA((8, parts))
    sems2 = pltpu.SemaphoreType.DMA((8, parts2))
    return pl.pallas_call(
        functools.partial(encode_kernel, parts, parts2),
        grid=(bricks // BLOCK,),
        out_shape=(
            jax.ShapeDtypeStruct((bricks, 3, 16, 128), BF16),
            jax.ShapeDtypeStruct((slots, 8, 128), BF16),
            jax.ShapeDtypeStruct((8, part, 3, 16, 128), BF16),
        ),
        in_specs=[SMEM, SMEM, SMEM, VMEM, VMEM, VMEM],
        out_specs=(pl.BlockSpec((BLOCK, 3, 16, 128), lambda i: (i, 0, 0, 0)), VMEM, ANY),
        scratch_shapes=[
            pltpu.VMEM((4, bricks + 8 * part + 1, 3, 16, 128), BF16),
            pltpu.VMEM((bricks + 1, 8, 128), F32),
            pltpu.VMEM((part, 3, 16, 128), BF16),
            pltpu.VMEM((TAPS + 1, 96, 128), BF16),
            pltpu.VMEM((wd.shape[0] // 2, 256), BF16),
            sems, sems, sems2, sems2,
        ],
        compiler_params=pltpu.CompilerParams(
            vmem_limit_bytes=56 * MIB, collective_id=1, has_side_effects=True
        ),
        name="encode",
    )(table, count, send_slot, w, wd, x)


def raw_kernel(table, w_in, own, halo_ref, after, out_ref, rot, w_ref, sems):
    step = pl.program_id(0)
    bricks = own.shape[0]
    part = halo_ref.shape[1]
    total = bricks + 8 * part
    side = Exchange(None, None, None, None, 1)

    @pl.when(step == 0)
    def _():
        mine = pltpu.make_async_copy(own, rot.at[0, pl.ds(0, bricks)], sems.at[8])
        mine.start()
        widen(w_ref, w_in)
        piece = lambda slot: pltpu.make_async_copy(
            halo_ref.at[slot], rot.at[0, pl.ds(bricks + slot * part, part)], sems.at[slot]
        )
        for slot in range(8):

            @pl.when(side.has(*OFFSETS[slot]))
            def _():
                piece(slot).start()

        for j in range(4):
            rot[j, total] = jnp.zeros((3, 16, 128), BF16)
        mine.wait()
        rotate_range(rot, 0, bricks)
        for slot in range(8):
            here = side.has(*OFFSETS[slot])

            @pl.when(here)
            def _():
                piece(slot).wait()

            @pl.when(jnp.logical_not(here))
            def _():
                def clear(n, carry):
                    rot[0, bricks + slot * part + n] = jnp.zeros((3, 16, 128), BF16)
                    return carry

                lax.fori_loop(0, part, clear, 0)

        rotate_range(rot, bricks, total)

    for u, tile in enumerate(conv_block(step, table, w_ref, rot)):
        out_ref[:, u] = tile.reshape(BLOCK, 16, 128)


def raw_conv(table, w, own, halos, after):
    bricks = own.shape[0]
    total = bricks + 8 * halos.shape[1]
    return pl.pallas_call(
        raw_kernel,
        grid=(bricks // BLOCK,),
        out_shape=jax.ShapeDtypeStruct((bricks, 3, 16, 128), F32),
        in_specs=[SMEM, VMEM, ANY, ANY, ANY],
        out_specs=pl.BlockSpec((BLOCK, 3, 16, 128), lambda i: (i, 0, 0, 0)),
        scratch_shapes=[
            pltpu.VMEM((4, total + 1, 3, 16, 128), BF16),
            pltpu.VMEM((TAPS + 1, 96, 128), BF16),
            pltpu.SemaphoreType.DMA((9,)),
        ],
        compiler_params=pltpu.CompilerParams(vmem_limit_bytes=56 * MIB),
        cost_estimate=pl.CostEstimate(flops=40_000_000_000, bytes_accessed=13_000_000, transcendentals=0),
        name="raw_conv",
    )(table, w, own, halos, after)


def coarse_kernel(from_slot, to_place, w_in, in_ref, after, out_ref, cells, grid, turned, w_ref):
    places = from_slot.shape[0]
    groups = places // 8
    grid[...] = jnp.zeros(grid.shape, BF16)
    widen(w_ref, w_in)

    def land(p, carry):
        cells[pl.ds(pl.multiple_of(p * 8, 8), 8)] = in_ref[from_slot[p]].astype(F32)
        return carry

    lax.fori_loop(0, places, land, 0, unroll=8)
    voxels = list(itertools.product(range(4), repeat=3))

    def base(z, y, x):
        t = (z // 2) * 4 + (y // 2) * 2 + x // 2
        c = (z % 2) * 4 + (y % 2) * 2 + x % 2
        return t * places + c

    zero = jnp.zeros((32 - groups, 128), F32)
    for z, y, x in voxels:
        piece = cells[pl.ds(base(z, y, x), groups, stride=8)]
        grid[z + 1, y + 1, x + 1] = jnp.concatenate([piece, zero], axis=0).astype(BF16)

    for z in range(4):
        acc = None
        for k0 in range(0, TAPS + 1, 2):
            sides = []
            for k in (k0, min(k0 + 1, TAPS - 1)):
                dz, dy, dx = k // 9, k // 3 % 3, k % 3
                sides.append(grid[z + dz, dy : dy + 4, dx : dx + 4].reshape(16 * 32, 128))
            rhs = jnp.concatenate([w_ref[k0], w_ref[k0 + 1]], axis=0)
            part = jnp.dot(jnp.concatenate(sides, axis=1), rhs, preferred_element_type=F32)
            acc = part if acc is None else acc + part
        acc = acc.reshape(16, 32, 128)
        for y in range(4):
            for x in range(4):
                here = grid[z + 1, y + 1, x + 1].astype(F32) + jnp.maximum(acc[y * 4 + x], 0.0)
                turned[pl.ds(base(z, y, x), groups, stride=8)] = here[:groups]
    turned[pl.ds(places * 8, 8)] = jnp.zeros((8, 128), F32)

    def reply(s, carry):
        out_ref[s] = turned[pl.ds(pl.multiple_of(to_place[s] * 8, 8), 8)].astype(BF16)
        return carry

    lax.fori_loop(0, out_ref.shape[0], reply, 0, unroll=8)


def coarse(from_slot, to_place, w, incoming, after):
    places = from_slot.shape[0]
    return pl.pallas_call(
        coarse_kernel,
        out_shape=jax.ShapeDtypeStruct(incoming.shape, BF16),
        in_specs=[SMEM, SMEM, VMEM, VMEM, ANY],
        out_specs=VMEM,
        scratch_shapes=[
            pltpu.VMEM((places * 8, 128), F32),
            pltpu.VMEM((6, 6, 6, 32, 128), BF16),
            pltpu.VMEM((places * 8 + 8, 128), F32),
            pltpu.VMEM((TAPS + 1, 128, 128), BF16),
        ],
        compiler_params=pltpu.CompilerParams(vmem_limit_bytes=32 * MIB),
        name="coarse_mix",
    )(from_slot, to_place, w, incoming, after)


def spread_kernel(slot, count, in_ref, out_ref, face, landed, sends, recvs):
    bricks = slot.shape[0]
    part = bricks // 4
    ring = Exchange(lambda c: face, lambda k, c: landed.at[k], sends, recvs, 1)
    ring.greet()

    def take(b, carry):
        value = in_ref[slot[b]].astype(F32)
        out_ref[b] = jnp.where(b < count[0], value, 0.0)
        return carry

    lax.fori_loop(0, part, take, 0, unroll=8)
    face[...] = out_ref[pl.ds(0, part)].reshape(face.shape).astype(BF16)
    ring.meet()
    ring.start(0)
    lax.fori_loop(part, bricks, take, 0, unroll=8)
    out_ref[bricks + 8 * part] = jnp.zeros((8, 128), F32)
    ring.forward(0)
    for k in (3, 4, 1, 6, 0, 2, 5, 7):
        begin = bricks + k * part
        here = ring.has(*OFFSETS[k])
        if OFFSETS[k][1]:
            ring.arrive(k)

        @pl.when(here)
        def _():
            out_ref[pl.ds(begin, part)] = landed[k].astype(F32).reshape(part, 8, 128)

        @pl.when(jnp.logical_not(here))
        def _():
            out_ref[pl.ds(begin, part)] = jnp.zeros((part, 8, 128), F32)

    ring.finish()


def spread(slot, count, returned):
    bricks = slot.shape[0]
    part = bricks // 4
    return pl.pallas_call(
        spread_kernel,
        out_shape=jax.ShapeDtypeStruct((bricks + 8 * part + 1, 8, 128), F32),
        in_specs=[SMEM, SMEM, VMEM],
        out_specs=VMEM,
        scratch_shapes=[
            pltpu.VMEM((part // 2, 16, 128), BF16),
            pltpu.VMEM((8, part // 2, 16, 128), BF16),
            pltpu.SemaphoreType.DMA((8, 1)),
            pltpu.SemaphoreType.DMA((8, 1)),
        ],
        compiler_params=pltpu.CompilerParams(
            vmem_limit_bytes=16 * MIB, collective_id=2, has_side_effects=True
        ),
        name="spread",
    )(slot, count, returned)


def merge_kernel(up_ref, w_in, out_ref, stack, wide):
    chans = up_ref.shape[0]
    out_ref[...] = jnp.zeros(out_ref.shape, BF16)
    wide[...] = jnp.zeros(wide.shape, BF16)
    for s in range(8):
        stack[s * chans : (s + 1) * chans] = up_ref[:, s * chans : (s + 1) * chans]
    lane = lax.broadcasted_iota(jnp.int32, (chans, 128), 1)

    def body(k, carry):
        wide[:, :chans] = w_in[k]
        whole = jnp.dot(stack[...], wide[...], preferred_element_type=F32)
        for h in range(2):
            a = [whole[(4 * h + i) * chans : (4 * h + i + 1) * chans] for i in range(4)]
            r1, r2, r3 = pltpu.roll(a[1], 96, 1), pltpu.roll(a[2], 64, 1), pltpu.roll(a[3], 32, 1)
            tiles = (jnp.where(lane < 96, a[0], r1), jnp.where(lane < 64, r1, r2), jnp.where(lane < 32, r2, r3))
            for u in range(3):
                out_ref[k, :chans, h * 384 + u * 128 : h * 384 + (u + 1) * 128] = tiles[u].astype(BF16)
        return carry

    lax.fori_loop(0, TAPS, body, 0)


def merge(w_up, w):
    chans = w_up.shape[0]
    return pl.pallas_call(
        merge_kernel,
        out_shape=jax.ShapeDtypeStruct((TAPS + 1, 128, 8 * chans), BF16),
        in_specs=[VMEM, VMEM],
        out_specs=VMEM,
        scratch_shapes=[pltpu.VMEM((8 * chans, chans), BF16), pltpu.VMEM((chans, 128), BF16)],
        compiler_params=pltpu.CompilerParams(vmem_limit_bytes=24 * MIB),
        cost_estimate=pl.CostEstimate(flops=8_000_000_000, bytes_accessed=8_000_000, transcendentals=0),
        name="merge",
    )(w_up, w)


def decode_kernel(table, count, w_ref, up_ref, cells, raw_ref, enc_ref, out_ref):
    step = pl.program_id(0)
    block = enc_ref.shape[0]
    acc = None
    for g in range(7):
        columns = []
        for j in range(4):
            k = 4 * g + j
            if k < TAPS:
                rows = [cells[table[k, step * block + b]] for b in range(block)]
                columns.append(jnp.concatenate(rows, axis=0).astype(BF16))
            else:
                columns.append(jnp.zeros((block * 8, 128), BF16))
        lhs = jnp.concatenate(columns, axis=1)
        part_sum = jnp.dot(lhs, w_ref[g * 512 : (g + 1) * 512], preferred_element_type=F32)
        acc = part_sum if acc is None else acc + part_sum
    mine = cells[pl.ds(step * block, block)].reshape(block * 8, 128).astype(BF16)
    up = jnp.concatenate([up_ref[...], jnp.zeros((128 - up_ref.shape[0], up_ref.shape[1]), BF16)], axis=0)
    lifted = jnp.dot(mine, up, preferred_element_type=F32)
    live = lax.broadcasted_iota(jnp.int32, (block, 8, 128), 0) + step * block < count[0]
    tiles = []
    for u in range(3):
        halves = []
        coded = enc_ref[:, u].astype(F32)
        for h in range(2):
            lanes = slice(h * 384 + u * 128, h * 384 + (u + 1) * 128)
            restored = coded[:, h * 8 : h * 8 + 8] + lifted[:, lanes].reshape(block, 8, 128)
            restored = restored.astype(BF16).astype(F32)
            mixed = raw_ref[:, u, h * 8 : h * 8 + 8] + acc[:, lanes].reshape(block, 8, 128)
            halves.append(jnp.where(live, restored + jnp.maximum(mixed, 0.0), 0.0))
        tiles.append(jnp.concatenate(halves, axis=1).astype(BF16))
    for b in range(0, block, 16):
        out_ref[b : b + 16] = from_dense([x[b : b + 16] for x in tiles])


def decode(table, count, w, up, cells, raw, enc, block=48):
    bricks = enc.shape[0]
    blocked = lambda: pl.BlockSpec((block, 3, 16, 128), lambda i: (i, 0, 0, 0))
    return pl.pallas_call(
        decode_kernel,
        grid=(bricks // block,),
        out_shape=jax.ShapeDtypeStruct((bricks, 6144), BF16),
        in_specs=[SMEM, SMEM, VMEM, VMEM, VMEM, blocked(), blocked()],
        out_specs=pl.BlockSpec((block, 6144), lambda i: (i, 0)),
        compiler_params=pltpu.CompilerParams(vmem_limit_bytes=48 * MIB),
        name="decode",
    )(table, count, w, up, cells, raw, enc)


def relay(buffer, devices):
    moved = lax.all_to_all(
        buffer.reshape(devices, -1, 128), ("gz", "gx"), split_axis=0, concat_axis=0, tiled=True
    )
    return moved.reshape(-1, 8, 128)


def on_device(
    features, active_count, neighbors, owner, arrival_cell, w_enc, w_down, w_mid, w_up, w_dec
):
    devices = lax.axis_size("gz") * lax.axis_size("gx")
    bricks = features.shape[1]
    boundary = bricks // 4
    capacity = arrival_cell.shape[1] // devices
    slot_count = devices * capacity
    count = active_count[0]
    n = neighbors[0]
    m = n - bricks
    side = m // boundary
    n = jnp.where(m >= 4 * boundary, jnp.where(side == 4, m - 4 * boundary, n - boundary), n)
    empty = bricks + 8 * boundary
    table = jnp.where(n < 0, empty, n)
    target = owner[0]
    index = jnp.arange(bricks, dtype=jnp.int32)
    same = jnp.logical_and(target[:, None] == target[None, :], index[None, :] < index[:, None])
    slot = target * capacity + jnp.sum(same.astype(jnp.int32), axis=1)
    slot_ids = jnp.arange(slot_count, dtype=jnp.int32)
    send_slot = jnp.min(jnp.where(slot_ids[:, None] == slot[None, :], index[None, :], bricks), axis=1)
    arrivals = arrival_cell[0]
    to_place = jnp.where(arrivals < 0, bricks, arrivals % 8 * (bricks // 8) + arrivals // 8)
    from_slot = jnp.sum(
        jnp.where(index[:, None] == to_place[None, :], slot_ids[None, :], 0), axis=1
    )
    encoded, outgoing, encoded_halo = encode(table, count, send_slot, w_enc, w_down, features[0])
    incoming = relay(outgoing, devices)
    lift = merge(w_up, w_dec)
    reply = coarse(from_slot, to_place, w_mid, incoming, lift)
    returned = relay(reply, devices)
    raw = raw_conv(table, w_dec, encoded, encoded_halo, reply)
    cells = spread(slot, count, returned)
    decoded = decode(table, count, lift.reshape(-1, lift.shape[2]), w_up, cells, raw, encoded)
    return decoded[None]


def solution(mesh):
    placed = (
        P("gz", "gx", None),
        P("gz", "gx"),
        P("gz", None, "gx"),
        P("gz", "gx"),
        P("gz", "gx"),
        P(),
        P(),
        P(),
        P(),
        P(),
    )
    return jax.shard_map(
        on_device, mesh=mesh, in_specs=placed, out_specs=P("gz", "gx", None), check_vma=False
    )
```

```python
import functools
import itertools

import jax
import jax.numpy as jnp
from jax import lax
from jax.experimental import pallas as pl
from jax.experimental.pallas import tpu as pltpu
from jax.sharding import PartitionSpec as P

TAPS = 27
ORDER = [[(q - i) % 4 for q in range(4)] for i in range(4)]
CUT = (96, 64, 32)
BLOCK = 32
CHUNKS = ((0, 1), (2, 3), (4, 5), (6,))
MIB = 1024 * 1024
BF16 = jnp.bfloat16
F32 = jnp.float32


def swap_halves(a, b):
    low = lax.broadcasted_iota(jnp.int32, a[0].shape, a[0].ndim - 1) < 64
    turn = lambda x: pltpu.roll(x, 64, x.ndim - 1)
    a1, a2, b0, b1 = turn(a[1]), turn(a[2]), turn(b[0]), turn(b[1])
    first = (a[0], jnp.where(low, a[1], b0), jnp.where(low, b0, b1))
    second = (jnp.where(low, a1, a2), jnp.where(low, a2, b[1]), b[2])
    return first, second


def group_of(cz, sz, cy):
    return ((cz * 2 + sz) * 2 + cy) * 2, sz * 8 + cz * 4 + cy * 2


def to_dense(x):
    rows = [None] * 16
    for cz, sz, cy in itertools.product(range(2), repeat=3):
        g, r = group_of(cz, sz, cy)
        part = lambda s: [x[:, (g + s) * 384 + t * 128 : (g + s) * 384 + (t + 1) * 128] for t in range(3)]
        rows[r], rows[r + 1] = swap_halves(part(0), part(1))
    return [jnp.swapaxes(jnp.stack([row[t] for row in rows], axis=0), 0, 1) for t in range(3)]


def from_dense(tiles):
    rows = [jnp.swapaxes(x, 0, 1) for x in tiles]
    out = [None] * 16
    for cz, sz, cy in itertools.product(range(2), repeat=3):
        g, r = group_of(cz, sz, cy)
        out[g], out[g + 1] = swap_halves([x[r] for x in rows], [x[r + 1] for x in rows])
    return jnp.concatenate([y for x in out for y in x], axis=1)


OFFSETS = tuple((dz, dx) for dz in (-1, 0, 1) for dx in (-1, 0, 1) if (dz, dx) != (0, 0))
MESH = pl.DeviceIdType.MESH


class Exchange:
    def __init__(self, own, landing, send, recv, chunks):
        self.own, self.landing, self.send, self.recv, self.chunks = own, landing, send, recv, chunks
        self.z, self.x = lax.axis_index("gz"), lax.axis_index("gx")
        self.layers, self.slabs = lax.axis_size("gz"), lax.axis_size("gx")

    def has(self, dz, dx):
        checks = []
        if dz:
            checks.append(self.z > 0 if dz < 0 else self.z < self.layers - 1)
        if dx:
            checks.append(self.x > 0 if dx < 0 else self.x < self.slabs - 1)
        return checks[0] if len(checks) == 1 else jnp.logical_and(*checks)

    def sends(self, slot):
        dz, dx = OFFSETS[slot]
        if dz and dx:
            sides = [self.z > 0 if dz < 0 else self.z < self.layers - 1]
            sides.append(self.x < self.slabs - 1 if dx < 0 else self.x > 0)
            return jnp.logical_and(*sides)
        return self.has(-dz, -dx)

    def copy(self, slot, c):
        dz, dx = OFFSETS[slot]
        if dz and dx:
            source, target = self.landing(OFFSETS.index((dz, 0)), c), (self.z, self.x - dx)
        else:
            source, target = self.own(c), (self.z - dz, self.x - dx)
        return pltpu.make_async_remote_copy(
            src_ref=source,
            dst_ref=self.landing(slot, c),
            send_sem=self.send.at[slot, c],
            recv_sem=self.recv.at[slot, c],
            device_id=target,
            device_id_type=MESH,
        )

    def greet(self):
        barrier = pltpu.get_barrier_semaphore()
        for dz, dx in ((-1, 0), (1, 0), (0, -1), (0, 1)):

            @pl.when(self.has(dz, dx))
            def _():
                pl.semaphore_signal(
                    barrier, inc=1, device_id=(self.z + dz, self.x + dx), device_id_type=MESH
                )

    def meet(self):
        peers = sum(self.has(dz, dx).astype(jnp.int32) for dz, dx in ((-1, 0), (1, 0), (0, -1), (0, 1)))
        pl.semaphore_wait(pltpu.get_barrier_semaphore(), peers)

    def start(self, *chunks):
        for c in chunks:
            for slot in (1, 6, 3, 4):

                @pl.when(self.sends(slot))
                def _():
                    self.copy(slot, c).start()

    def forward(self, c):
        for slot, corners in ((1, (0, 2)), (6, (5, 7))):

            @pl.when(self.has(*OFFSETS[slot]))
            def _():
                self.copy(slot, c).wait_recv()

            for corner in corners:

                @pl.when(self.sends(corner))
                def _():
                    self.copy(corner, c).start()

    def arrive(self, slot):
        @pl.when(self.has(*OFFSETS[slot]))
        def _():
            for c in range(self.chunks):
                self.copy(slot, c).wait_recv()

    def finish(self):
        for slot in range(8):

            @pl.when(self.sends(slot))
            def _():
                for c in range(self.chunks):
                    self.copy(slot, c).wait_send()


def rotate_range(rot, start, stop, size=48):
    rows = size * 16
    wide = lax.broadcasted_iota(jnp.int32, (rows, 128), 1)
    source = lax.broadcasted_iota(jnp.int32, (128, 384), 0)
    lane = lax.broadcasted_iota(jnp.int32, (128, 384), 1)
    shift = jnp.where(lane < 128, 96, jnp.where(lane < 256, 64, 32))
    turn = (source == ((lane - shift) & 127)).astype(F32).astype(BF16)

    def body(m, carry):
        n = pl.multiple_of(start + m * size, 16)
        tiles = [rot[0, pl.ds(n, size), t].reshape(rows, 128) for t in range(3)]
        turned = jnp.dot(tiles[0], turn, preferred_element_type=F32).astype(BF16)
        done = []
        for j in range(1, 4):
            amount = (96 * j) % 128
            rolled = [turned[:, (j - 1) * 128 : j * 128]]
            rolled += [pltpu.roll(x, amount, 1) for x in tiles[1:]]
            for u in range(3):
                hi = (128 * u + 127 - 96 * j) // 128 % 3
                lo = (128 * u - 96 * j) // 128 % 3
                done.append((j, u, jnp.where(wide >= amount, rolled[hi], rolled[lo]).reshape(size, 16, 128)))
        for j, u, x in done:
            rot[j, pl.ds(n, size), u] = x
        return carry

    lax.fori_loop(0, (stop - start) // size, body, 0)


def widen(wide, w_ref):
    wide[...] = jnp.zeros(wide.shape, BF16)
    for k in range(w_ref.shape[0]):
        wide[k, : w_ref.shape[1], : w_ref.shape[2]] = w_ref[k]


def conv_block(step, table, w_ref, rot):
    lane = lax.broadcasted_iota(jnp.int32, (16, 128), 1)

    def gather(c, b):
        brick = step * BLOCK + b
        lanes = [[] for _ in range(4)]
        for g in CHUNKS[c]:
            loads = []
            for j in range(4):
                if 4 * g + j < TAPS:
                    n = table[4 * g + j, brick]
                    loads.append([rot[j, n, t] for t in range(3)])
                else:
                    loads.append([jnp.zeros((16, 128), BF16)] * 3)
            for i in range(4):
                for u in range(3):
                    a, b2 = loads[ORDER[i][u]][u], loads[ORDER[i][u + 1]][u]
                    lanes[i].append(jnp.where(lane < CUT[u], a, b2))
        return lanes

    acc = [None] * 4
    for c in range(len(CHUNKS)):
        got = [gather(c, b) for b in range(BLOCK)]
        for i in range(4):
            lhs = jnp.concatenate([jnp.concatenate(x[i], axis=1) for x in got], axis=0)
            taps = [4 * g + ORDER[i][q] for g in CHUNKS[c] for q in range(4)]
            rhs = jnp.concatenate([w_ref[k] for k in taps], axis=0)
            part = jnp.dot(lhs, rhs, preferred_element_type=F32)
            acc[i] = part if acc[i] is None else acc[i] + part
    r1 = pltpu.roll(acc[1], 96, 1)
    r2 = pltpu.roll(acc[2], 64, 1)
    r3 = pltpu.roll(acc[3], 32, 1)
    lanes = lax.broadcasted_iota(jnp.int32, acc[0].shape, 1)
    return (jnp.where(lanes < 96, acc[0], r1), jnp.where(lanes < 64, r1, r2), jnp.where(lanes < 32, r2, r3))


def encode_kernel(
    parts, parts2, table, count, send_slot, w_in, wd_in, x_ref,
    enc_ref, out_ref, halo_ref, rot, pooled, face, w_ref, wd_ref, sends, recvs, sends2, recvs2,
):
    step = pl.program_id(0)
    bricks = x_ref.shape[0]
    part = bricks // 4
    size = part // parts
    size2 = part // parts2
    total = bricks + 8 * part
    first = Exchange(
        lambda c: rot.at[0, pl.ds(c * size, size)],
        lambda slot, c: rot.at[0, pl.ds(bricks + slot * part + c * size, size)],
        sends, recvs, parts,
    )
    second = Exchange(
        lambda c: face.at[pl.ds(c * size2, size2)],
        lambda slot, c: halo_ref.at[slot, pl.ds(c * size2, size2)],
        sends2, recvs2, parts2,
    )

    def fill(slot):
        begin = bricks + slot * part
        first.arrive(slot) if OFFSETS[slot][1] else None

        @pl.when(jnp.logical_not(first.has(*OFFSETS[slot])))
        def _():
            def clear(n, carry):
                rot[0, begin + n] = jnp.zeros((3, 16, 128), BF16)
                return carry

            lax.fori_loop(0, part, clear, 0)

        rotate_range(rot, begin, begin + part)

    def densify(start, stop):
        def body(m, carry):
            begin = pl.multiple_of(m * 16, 16)
            x = x_ref[pl.ds(begin, 16)]
            live = lax.broadcasted_iota(jnp.int32, x.shape, 0) + begin < count[0]
            for t, y in enumerate(to_dense(jnp.where(live, x, jnp.zeros((), BF16)))):
                rot[0, pl.ds(begin, 16), t] = y
            return carry

        lax.fori_loop(start // 16, stop // 16, body, 0)

    @pl.when(step == 0)
    def _():
        first.greet()
        densify(0, part)
        first.meet()
        first.start(*range(parts))
        for j in range(4):
            rot[j, total] = jnp.zeros((3, 16, 128), BF16)
        pooled[bricks] = jnp.zeros((8, 128), F32)
        widen(w_ref, w_in)
        wd_ref[...] = jnp.zeros(wd_ref.shape, BF16)
        half, chans = wd_in.shape[0] // 2, wd_in.shape[1]
        wd_ref[:, :chans] = wd_in[:half]
        wd_ref[:, 128 : 128 + chans] = wd_in[half:]
        densify(part, 2 * part)
        first.forward(0)
        densify(2 * part, 3 * part)
        first.forward(1)
        densify(3 * part, bricks)
        first.forward(2)
        rotate_range(rot, 0, 2 * part)
        first.forward(3)
        rotate_range(rot, 2 * part, bricks)
        first.forward(4)
        fill(3)
        fill(4)
        first.forward(5)
        for slot in (1, 6, 0, 2, 5, 7):
            fill(slot)
        first.finish()

    tiles = conv_block(step, table, w_ref, rot)
    shape = tiles[0].shape
    live = lax.broadcasted_iota(jnp.int32, shape, 0) // 16 + step * BLOCK < count[0]
    values = []
    for u in range(3):
        mine = rot[0, pl.ds(step * BLOCK, BLOCK), u].reshape(shape).astype(F32)
        value = jnp.where(live, mine + jnp.maximum(tiles[u], 0.0), 0.0).astype(BF16)
        enc_ref[:, u] = value.reshape(BLOCK, 16, 128)
        values.append(value)
    sums = jnp.dot(jnp.concatenate(values, axis=1), wd_ref[...], preferred_element_type=F32)
    sums = sums.reshape(BLOCK, 16, 256)
    sums = sums[:, :8, :128] + sums[:, 8:, 128:]
    pooled[pl.ds(step * BLOCK, BLOCK)] = sums

    @pl.when(step == 0)
    def _():
        face[pl.ds(0, BLOCK)] = enc_ref[...]
        second.start(0, 1)

    @pl.when(step == 1)
    def _():
        face[pl.ds(BLOCK, part - BLOCK)] = enc_ref[: part - BLOCK]
        second.start(2)

    @pl.when(step == 2)
    def _():
        second.forward(0)

    @pl.when(step == 3)
    def _():
        second.forward(1)
        second.forward(2)

    @pl.when(step == pl.num_programs(0) - 1)
    def _():
        def place(s, carry):
            out_ref[s] = pooled[send_slot[s]].astype(BF16)
            return carry

        lax.fori_loop(0, out_ref.shape[0], place, 0, unroll=8)
        for slot in (0, 2, 3, 4, 5, 7):
            second.arrive(slot)
        second.finish()


def field_scratch(own, halos):
    total = own.shape[0] + len(halos) * halos[0].shape[0]
    return pltpu.VMEM((4, total + 1, 3, 16, 128), BF16)


SMEM = pl.BlockSpec(memory_space=pltpu.SMEM)
VMEM = pl.BlockSpec(memory_space=pltpu.VMEM)
ANY = pl.BlockSpec(memory_space=pl.ANY)


def encode(table, count, send_slot, w, wd, x):
    bricks = x.shape[0]
    part = bricks // 4
    slots = send_slot.shape[0]
    parts, parts2 = 6, 3
    sems = pltpu.SemaphoreType.DMA((8, parts))
    sems2 = pltpu.SemaphoreType.DMA((8, parts2))
    return pl.pallas_call(
        functools.partial(encode_kernel, parts, parts2),
        grid=(bricks // BLOCK,),
        out_shape=(
            jax.ShapeDtypeStruct((bricks, 3, 16, 128), BF16),
            jax.ShapeDtypeStruct((slots, 8, 128), BF16),
            jax.ShapeDtypeStruct((8, part, 3, 16, 128), BF16),
        ),
        in_specs=[SMEM, SMEM, SMEM, VMEM, VMEM, VMEM],
        out_specs=(pl.BlockSpec((BLOCK, 3, 16, 128), lambda i: (i, 0, 0, 0)), VMEM, ANY),
        scratch_shapes=[
            pltpu.VMEM((4, bricks + 8 * part + 1, 3, 16, 128), BF16),
            pltpu.VMEM((bricks + 1, 8, 128), F32),
            pltpu.VMEM((part, 3, 16, 128), BF16),
            pltpu.VMEM((TAPS + 1, 96, 128), BF16),
            pltpu.VMEM((wd.shape[0] // 2, 256), BF16),
            sems, sems, sems2, sems2,
        ],
        compiler_params=pltpu.CompilerParams(
            vmem_limit_bytes=56 * MIB, collective_id=1, has_side_effects=True
        ),
        name="encode",
    )(table, count, send_slot, w, wd, x)


def coarse_mix(from_slot, to_place, w_ref, in_ref, out_ref, cells, grid, turned, mixed):
    places = from_slot.shape[0]
    groups = places // 8

    def land(p, carry):
        cells[pl.ds(pl.multiple_of(p * 8, 8), 8)] = in_ref[from_slot[p]].astype(F32)
        return carry

    lax.fori_loop(0, places, land, 0, unroll=8)
    voxels = list(itertools.product(range(4), repeat=3))

    def base(z, y, x):
        t = (z // 2) * 4 + (y // 2) * 2 + x // 2
        c = (z % 2) * 4 + (y % 2) * 2 + x % 2
        return t * places + c

    zero = jnp.zeros((32 - groups, 128), F32)
    for z, y, x in voxels:
        piece = cells[pl.ds(base(z, y, x), groups, stride=8)]
        grid[z + 1, y + 1, x + 1] = jnp.concatenate([piece, zero], axis=0).astype(BF16)

    for z in range(4):
        acc = None
        for k0 in range(0, TAPS + 1, 2):
            sides = []
            for k in (k0, min(k0 + 1, TAPS - 1)):
                dz, dy, dx = k // 9, k // 3 % 3, k % 3
                sides.append(grid[z + dz, dy : dy + 4, dx : dx + 4].reshape(16 * 32, 128))
            rhs = jnp.concatenate([w_ref[k0], w_ref[k0 + 1]], axis=0)
            part = jnp.dot(jnp.concatenate(sides, axis=1), rhs, preferred_element_type=F32)
            acc = part if acc is None else acc + part
        acc = acc.reshape(16, 32, 128)
        for y in range(4):
            for x in range(4):
                here = grid[z + 1, y + 1, x + 1].astype(F32) + jnp.maximum(acc[y * 4 + x], 0.0)
                turned[pl.ds(base(z, y, x), groups, stride=8)] = here[:groups]
    mixed[pl.ds(0, places)] = turned[...].reshape(places, 8, 128)
    mixed[places] = jnp.zeros((8, 128), F32)

    def reply(s, carry):
        out_ref[s] = mixed[to_place[s]].astype(BF16)
        return carry

    lax.fori_loop(0, out_ref.shape[0], reply, 0, unroll=8)


def each_peer(act):
    layers, slabs = lax.axis_size("gz"), lax.axis_size("gx")
    devices = layers * slabs
    me = lax.axis_index("gz") * slabs + lax.axis_index("gx")

    def body(i, carry):
        d = (me + i) % devices
        act(d, (d // slabs, d % slabs))
        return carry

    lax.fori_loop(1, devices, body, 0)


class Relay:
    def __init__(self, source, landing, sems):
        self.source, self.landing, self.sems = source, landing, sems
        self.slabs = lax.axis_size("gx")
        self.devices = lax.axis_size("gz") * self.slabs
        self.me = lax.axis_index("gz") * self.slabs + lax.axis_index("gx")
        self.cap = source.shape[0] // self.devices

    def copy(self, begin, end, rows, peer):
        return pltpu.make_async_remote_copy(
            src_ref=self.source.at[pl.ds(begin, rows)],
            dst_ref=self.landing.at[pl.ds(end, rows)],
            send_sem=self.sems.at[0],
            recv_sem=self.sems.at[1],
            device_id=peer,
            device_id_type=MESH,
        )

    def start(self):
        each_peer(lambda d, peer: self.copy(d * self.cap, self.me * self.cap, self.cap, peer).start())
        mine = pl.ds(self.me * self.cap, self.cap)
        self.landing[mine] = self.source[mine]

    def wait(self):
        peer = (self.me + 1) % self.devices
        whole = self.copy(0, 0, self.cap * (self.devices - 1), (peer // self.slabs, peer % self.slabs))
        whole.wait_recv()
        whole.wait_send()


def middle_kernel(
    table, count, from_slot, to_place, slot, w_dec, w_mid, w_up, outgoing, own, halo_ref,
    raw_ref, field, lift, rot, w_ref, wm_ref, stack, wide, incoming, reply, returned,
    cells, grid, turned, mixed, face, landed, local, relays, sends, recvs,
):
    step = pl.program_id(0)
    bricks = own.shape[0]
    part = bricks // 4
    total = bricks + 8 * part
    ring = Exchange(lambda c: face, lambda k, c: landed.at[k], sends, recvs, 1)
    out = Relay(outgoing, incoming, relays.at[0])
    back = Relay(reply, returned, relays.at[1])

    @pl.when(step == 0)
    def _():
        barrier = pltpu.get_barrier_semaphore()
        each_peer(
            lambda d, peer: pl.semaphore_signal(barrier, inc=1, device_id=peer, device_id_type=MESH)
        )
        mine = pltpu.make_async_copy(own, rot.at[0, pl.ds(0, bricks)], local.at[8])
        mine.start()
        piece = lambda k: pltpu.make_async_copy(
            halo_ref.at[k], rot.at[0, pl.ds(bricks + k * part, part)], local.at[k]
        )
        for k in range(8):

            @pl.when(ring.has(*OFFSETS[k]))
            def _():
                piece(k).start()

        pl.semaphore_wait(barrier, out.devices - 1)
        out.start()
        for j in range(4):
            rot[j, total] = jnp.zeros((3, 16, 128), BF16)
        widen(w_ref, w_dec)
        widen(wm_ref, w_mid)
        grid[...] = jnp.zeros(grid.shape, BF16)
        mine.wait()
        rotate_range(rot, 0, bricks)
        for k in range(8):
            here = ring.has(*OFFSETS[k])

            @pl.when(here)
            def _():
                piece(k).wait()

            @pl.when(jnp.logical_not(here))
            def _():
                def clear(n, carry):
                    rot[0, bricks + k * part + n] = jnp.zeros((3, 16, 128), BF16)
                    return carry

                lax.fori_loop(0, part, clear, 0)

        rotate_range(rot, bricks, total)
        merge_weights(w_up, w_dec, lift, stack, wide)
        out.wait()
        coarse_mix(from_slot, to_place, wm_ref, incoming, reply, cells, grid, turned, mixed)
        back.start()

    for u, tile in enumerate(conv_block(step, table, w_ref, rot)):
        raw_ref[:, u] = tile.reshape(BLOCK, 16, 128)

    def take(b, carry):
        value = returned[slot[b]].astype(F32)
        field[b] = jnp.where(b < count[0], value, 0.0)
        return carry

    @pl.when(step == 3)
    def _():
        back.wait()
        lax.fori_loop(0, part, take, 0, unroll=8)
        face[...] = field[pl.ds(0, part)].reshape(face.shape).astype(BF16)
        ring.start(0)
        lax.fori_loop(part, bricks, take, 0, unroll=8)
        field[total] = jnp.zeros((8, 128), F32)

    @pl.when(step == 4)
    def _():
        ring.forward(0)

    @pl.when(step == 5)
    def _():
        for k in (3, 4, 1, 6, 0, 2, 5, 7):
            begin = bricks + k * part
            here = ring.has(*OFFSETS[k])
            if OFFSETS[k][1]:
                ring.arrive(k)

            @pl.when(here)
            def _():
                field[pl.ds(begin, part)] = landed[k].astype(F32).reshape(part, 8, 128)

            @pl.when(jnp.logical_not(here))
            def _():
                field[pl.ds(begin, part)] = jnp.zeros((part, 8, 128), F32)

        ring.finish()


def middle(table, count, from_slot, to_place, slot, w_dec, w_mid, w_up, outgoing, own, halos):
    bricks = own.shape[0]
    part = bricks // 4
    total = bricks + 8 * part
    chans = w_up.shape[0]
    places = from_slot.shape[0]
    assert bricks == 6 * BLOCK
    relayed = pltpu.VMEM(outgoing.shape, BF16)
    return pl.pallas_call(
        middle_kernel,
        grid=(bricks // BLOCK,),
        out_shape=(
            jax.ShapeDtypeStruct((bricks, 3, 16, 128), F32),
            jax.ShapeDtypeStruct((total + 1, 8, 128), F32),
            jax.ShapeDtypeStruct((TAPS + 1, 128, 8 * chans), BF16),
        ),
        in_specs=[SMEM] * 5 + [VMEM] * 4 + [ANY, ANY],
        out_specs=(pl.BlockSpec((BLOCK, 3, 16, 128), lambda i: (i, 0, 0, 0)), VMEM, VMEM),
        scratch_shapes=[
            pltpu.VMEM((4, total + 1, 3, 16, 128), BF16),
            pltpu.VMEM((TAPS + 1, 96, 128), BF16),
            pltpu.VMEM((TAPS + 1, 128, 128), BF16),
            pltpu.VMEM((8 * chans, chans), BF16),
            pltpu.VMEM((chans, 128), BF16),
            relayed, relayed, relayed,
            pltpu.VMEM((places * 8, 128), F32),
            pltpu.VMEM((6, 6, 6, 32, 128), BF16),
            pltpu.VMEM((places * 8, 128), F32),
            pltpu.VMEM((places + 1, 8, 128), F32),
            pltpu.VMEM((part // 2, 16, 128), BF16),
            pltpu.VMEM((8, part // 2, 16, 128), BF16),
            pltpu.SemaphoreType.DMA((9,)),
            pltpu.SemaphoreType.DMA((2, 2)),
            pltpu.SemaphoreType.DMA((8, 1)),
            pltpu.SemaphoreType.DMA((8, 1)),
        ],
        compiler_params=pltpu.CompilerParams(
            vmem_limit_bytes=60 * MIB, collective_id=2, has_side_effects=True
        ),
        name="middle",
    )(table, count, from_slot, to_place, slot, w_dec, w_mid, w_up, outgoing, own, halos)


def merge_weights(up_ref, w_in, out_ref, stack, wide):
    chans = up_ref.shape[0]
    out_ref[...] = jnp.zeros(out_ref.shape, BF16)
    wide[...] = jnp.zeros(wide.shape, BF16)
    for s in range(8):
        stack[s * chans : (s + 1) * chans] = up_ref[:, s * chans : (s + 1) * chans]
    lane = lax.broadcasted_iota(jnp.int32, (chans, 128), 1)

    def body(k, carry):
        wide[:, :chans] = w_in[k]
        whole = jnp.dot(stack[...], wide[...], preferred_element_type=F32)
        for h in range(2):
            a = [whole[(4 * h + i) * chans : (4 * h + i + 1) * chans] for i in range(4)]
            r1, r2, r3 = pltpu.roll(a[1], 96, 1), pltpu.roll(a[2], 64, 1), pltpu.roll(a[3], 32, 1)
            tiles = (jnp.where(lane < 96, a[0], r1), jnp.where(lane < 64, r1, r2), jnp.where(lane < 32, r2, r3))
            for u in range(3):
                out_ref[k, :chans, h * 384 + u * 128 : h * 384 + (u + 1) * 128] = tiles[u].astype(BF16)
        return carry

    lax.fori_loop(0, TAPS, body, 0)


def decode_kernel(table, count, w_ref, up_ref, cells, raw_ref, enc_ref, out_ref):
    step = pl.program_id(0)
    block = enc_ref.shape[0]
    acc = None
    for g in range(7):
        columns = []
        for j in range(4):
            k = 4 * g + j
            if k < TAPS:
                rows = [cells[table[k, step * block + b]] for b in range(block)]
                columns.append(jnp.concatenate(rows, axis=0).astype(BF16))
            else:
                columns.append(jnp.zeros((block * 8, 128), BF16))
        lhs = jnp.concatenate(columns, axis=1)
        part_sum = jnp.dot(lhs, w_ref[g * 512 : (g + 1) * 512], preferred_element_type=F32)
        acc = part_sum if acc is None else acc + part_sum
    mine = cells[pl.ds(step * block, block)].reshape(block * 8, 128).astype(BF16)
    up = jnp.concatenate([up_ref[...], jnp.zeros((128 - up_ref.shape[0], up_ref.shape[1]), BF16)], axis=0)
    lifted = jnp.dot(mine, up, preferred_element_type=F32)
    live = lax.broadcasted_iota(jnp.int32, (block, 8, 128), 0) + step * block < count[0]
    tiles = []
    for u in range(3):
        halves = []
        coded = enc_ref[:, u].astype(F32)
        for h in range(2):
            lanes = slice(h * 384 + u * 128, h * 384 + (u + 1) * 128)
            restored = coded[:, h * 8 : h * 8 + 8] + lifted[:, lanes].reshape(block, 8, 128)
            restored = restored.astype(BF16).astype(F32)
            mixed = raw_ref[:, u, h * 8 : h * 8 + 8] + acc[:, lanes].reshape(block, 8, 128)
            halves.append(jnp.where(live, restored + jnp.maximum(mixed, 0.0), 0.0))
        tiles.append(jnp.concatenate(halves, axis=1).astype(BF16))
    for b in range(0, block, 16):
        out_ref[b : b + 16] = from_dense([x[b : b + 16] for x in tiles])


def decode(table, count, w, up, cells, raw, enc, block=48):
    bricks = enc.shape[0]
    blocked = lambda: pl.BlockSpec((block, 3, 16, 128), lambda i: (i, 0, 0, 0))
    return pl.pallas_call(
        decode_kernel,
        grid=(bricks // block,),
        out_shape=jax.ShapeDtypeStruct((bricks, 6144), BF16),
        in_specs=[SMEM, SMEM, VMEM, VMEM, VMEM, blocked(), blocked()],
        out_specs=pl.BlockSpec((block, 6144), lambda i: (i, 0)),
        compiler_params=pltpu.CompilerParams(vmem_limit_bytes=48 * MIB),
        name="decode",
    )(table, count, w, up, cells, raw, enc)


def relay(buffer, devices):
    moved = lax.all_to_all(
        buffer.reshape(devices, -1, 128), ("gz", "gx"), split_axis=0, concat_axis=0, tiled=True
    )
    return moved.reshape(-1, 8, 128)


def on_device(
    features, active_count, neighbors, owner, arrival_cell, w_enc, w_down, w_mid, w_up, w_dec
):
    devices = lax.axis_size("gz") * lax.axis_size("gx")
    bricks = features.shape[1]
    boundary = bricks // 4
    capacity = arrival_cell.shape[1] // devices
    slot_count = devices * capacity
    count = active_count[0]
    n = neighbors[0]
    m = n - bricks
    side = m // boundary
    n = jnp.where(m >= 4 * boundary, jnp.where(side == 4, m - 4 * boundary, n - boundary), n)
    empty = bricks + 8 * boundary
    table = jnp.where(n < 0, empty, n)
    target = owner[0]
    index = jnp.arange(bricks, dtype=jnp.int32)
    same = jnp.logical_and(target[:, None] == target[None, :], index[None, :] < index[:, None])
    slot = target * capacity + jnp.sum(same.astype(jnp.int32), axis=1)
    slot_ids = jnp.arange(slot_count, dtype=jnp.int32)
    send_slot = jnp.min(jnp.where(slot_ids[:, None] == slot[None, :], index[None, :], bricks), axis=1)
    arrivals = arrival_cell[0]
    to_place = jnp.where(arrivals < 0, bricks, arrivals % 8 * (bricks // 8) + arrivals // 8)
    from_slot = jnp.sum(
        jnp.where(index[:, None] == to_place[None, :], slot_ids[None, :], 0), axis=1
    )
    encoded, outgoing, encoded_halo = encode(table, count, send_slot, w_enc, w_down, features[0])
    raw, cells, lift = middle(
        table, count, from_slot, to_place, slot, w_dec, w_mid, w_up, outgoing, encoded, encoded_halo
    )
    decoded = decode(table, count, lift.reshape(-1, lift.shape[2]), w_up, cells, raw, encoded)
    return decoded[None]


def solution(mesh):
    placed = (
        P("gz", "gx", None),
        P("gz", "gx"),
        P("gz", None, "gx"),
        P("gz", "gx"),
        P("gz", "gx"),
        P(),
        P(),
        P(),
        P(),
        P(),
    )
    return jax.shard_map(
        on_device, mesh=mesh, in_specs=placed, out_specs=P("gz", "gx", None), check_vma=False
    )
```

```python
import functools
import itertools

import jax
import jax.numpy as jnp
from jax import lax
from jax.experimental import pallas as pl
from jax.experimental.pallas import tpu as pltpu
from jax.sharding import PartitionSpec as P

TAPS = 27
ORDER = [[(q - i) % 4 for q in range(4)] for i in range(4)]
CUT = (96, 64, 32)
BLOCK = 32
CHUNKS = ((0, 1), (2, 3), (4, 5), (6,))
MIB = 1024 * 1024
BF16 = jnp.bfloat16
F32 = jnp.float32


def swap_halves(a, b):
    low = lax.broadcasted_iota(jnp.int32, a[0].shape, a[0].ndim - 1) < 64
    turn = lambda x: pltpu.roll(x, 64, x.ndim - 1)
    a1, a2, b0, b1 = turn(a[1]), turn(a[2]), turn(b[0]), turn(b[1])
    first = (a[0], jnp.where(low, a[1], b0), jnp.where(low, b0, b1))
    second = (jnp.where(low, a1, a2), jnp.where(low, a2, b[1]), b[2])
    return first, second


def group_of(cz, sz, cy):
    return ((cz * 2 + sz) * 2 + cy) * 2, sz * 8 + cz * 4 + cy * 2


def to_dense(x):
    rows = [None] * 16
    for cz, sz, cy in itertools.product(range(2), repeat=3):
        g, r = group_of(cz, sz, cy)
        part = lambda s: [x[:, (g + s) * 384 + t * 128 : (g + s) * 384 + (t + 1) * 128] for t in range(3)]
        rows[r], rows[r + 1] = swap_halves(part(0), part(1))
    return [jnp.swapaxes(jnp.stack([row[t] for row in rows], axis=0), 0, 1) for t in range(3)]


def from_dense(tiles):
    rows = [jnp.swapaxes(x, 0, 1) for x in tiles]
    out = [None] * 16
    for cz, sz, cy in itertools.product(range(2), repeat=3):
        g, r = group_of(cz, sz, cy)
        out[g], out[g + 1] = swap_halves([x[r] for x in rows], [x[r + 1] for x in rows])
    return jnp.concatenate([y for x in out for y in x], axis=1)


OFFSETS = tuple((dz, dx) for dz in (-1, 0, 1) for dx in (-1, 0, 1) if (dz, dx) != (0, 0))
MESH = pl.DeviceIdType.MESH


class Exchange:
    def __init__(self, own, landing, send, recv, chunks):
        self.own, self.landing, self.send, self.recv, self.chunks = own, landing, send, recv, chunks
        self.z, self.x = lax.axis_index("gz"), lax.axis_index("gx")
        self.layers, self.slabs = lax.axis_size("gz"), lax.axis_size("gx")

    def has(self, dz, dx):
        checks = []
        if dz:
            checks.append(self.z > 0 if dz < 0 else self.z < self.layers - 1)
        if dx:
            checks.append(self.x > 0 if dx < 0 else self.x < self.slabs - 1)
        return checks[0] if len(checks) == 1 else jnp.logical_and(*checks)

    def sends(self, slot):
        dz, dx = OFFSETS[slot]
        if dz and dx:
            sides = [self.z > 0 if dz < 0 else self.z < self.layers - 1]
            sides.append(self.x < self.slabs - 1 if dx < 0 else self.x > 0)
            return jnp.logical_and(*sides)
        return self.has(-dz, -dx)

    def copy(self, slot, c):
        dz, dx = OFFSETS[slot]
        if dz and dx:
            source, target = self.landing(OFFSETS.index((dz, 0)), c), (self.z, self.x - dx)
        else:
            source, target = self.own(c), (self.z - dz, self.x - dx)
        return pltpu.make_async_remote_copy(
            src_ref=source,
            dst_ref=self.landing(slot, c),
            send_sem=self.send.at[slot, c],
            recv_sem=self.recv.at[slot, c],
            device_id=target,
            device_id_type=MESH,
        )

    def greet(self):
        barrier = pltpu.get_barrier_semaphore()
        for dz, dx in ((-1, 0), (1, 0), (0, -1), (0, 1)):

            @pl.when(self.has(dz, dx))
            def _():
                pl.semaphore_signal(
                    barrier, inc=1, device_id=(self.z + dz, self.x + dx), device_id_type=MESH
                )

    def meet(self):
        peers = sum(self.has(dz, dx).astype(jnp.int32) for dz, dx in ((-1, 0), (1, 0), (0, -1), (0, 1)))
        pl.semaphore_wait(pltpu.get_barrier_semaphore(), peers)

    def start(self, *chunks):
        for c in chunks:
            for slot in (1, 6, 3, 4):

                @pl.when(self.sends(slot))
                def _():
                    self.copy(slot, c).start()

    def forward(self, c):
        for slot, corners in ((1, (0, 2)), (6, (5, 7))):

            @pl.when(self.has(*OFFSETS[slot]))
            def _():
                self.copy(slot, c).wait_recv()

            for corner in corners:

                @pl.when(self.sends(corner))
                def _():
                    self.copy(corner, c).start()

    def arrive(self, slot):
        @pl.when(self.has(*OFFSETS[slot]))
        def _():
            for c in range(self.chunks):
                self.copy(slot, c).wait_recv()

    def finish(self):
        for slot in range(8):

            @pl.when(self.sends(slot))
            def _():
                for c in range(self.chunks):
                    self.copy(slot, c).wait_send()


def rotate_range(rot, start, stop, size=48):
    rows = size * 16
    wide = lax.broadcasted_iota(jnp.int32, (rows, 128), 1)
    source = lax.broadcasted_iota(jnp.int32, (128, 384), 0)
    lane = lax.broadcasted_iota(jnp.int32, (128, 384), 1)
    shift = jnp.where(lane < 128, 96, jnp.where(lane < 256, 64, 32))
    turn = (source == ((lane - shift) & 127)).astype(F32).astype(BF16)

    def body(m, carry):
        n = pl.multiple_of(start + m * size, 16)
        tiles = [rot[0, pl.ds(n, size), t].reshape(rows, 128) for t in range(3)]
        turned = jnp.dot(tiles[0], turn, preferred_element_type=F32).astype(BF16)
        done = []
        for j in range(1, 4):
            amount = (96 * j) % 128
            rolled = [turned[:, (j - 1) * 128 : j * 128]]
            rolled += [pltpu.roll(x, amount, 1) for x in tiles[1:]]
            for u in range(3):
                hi = (128 * u + 127 - 96 * j) // 128 % 3
                lo = (128 * u - 96 * j) // 128 % 3
                done.append((j, u, jnp.where(wide >= amount, rolled[hi], rolled[lo]).reshape(size, 16, 128)))
        for j, u, x in done:
            rot[j, pl.ds(n, size), u] = x
        return carry

    lax.fori_loop(0, (stop - start) // size, body, 0)


def widen(wide, w_ref):
    wide[...] = jnp.zeros(wide.shape, BF16)
    for k in range(w_ref.shape[0]):
        wide[k, : w_ref.shape[1], : w_ref.shape[2]] = w_ref[k]


def conv_block(step, table, w_ref, rot):
    lane = lax.broadcasted_iota(jnp.int32, (16, 128), 1)

    def gather(c, b):
        brick = step * BLOCK + b
        lanes = [[] for _ in range(4)]
        for g in CHUNKS[c]:
            loads = []
            for j in range(4):
                if 4 * g + j < TAPS:
                    n = table[4 * g + j, brick]
                    loads.append([rot[j, n, t] for t in range(3)])
                else:
                    loads.append([jnp.zeros((16, 128), BF16)] * 3)
            for i in range(4):
                for u in range(3):
                    a, b2 = loads[ORDER[i][u]][u], loads[ORDER[i][u + 1]][u]
                    lanes[i].append(jnp.where(lane < CUT[u], a, b2))
        return lanes

    acc = [None] * 4
    for c in range(len(CHUNKS)):
        got = [gather(c, b) for b in range(BLOCK)]
        for i in range(4):
            lhs = jnp.concatenate([jnp.concatenate(x[i], axis=1) for x in got], axis=0)
            taps = [4 * g + ORDER[i][q] for g in CHUNKS[c] for q in range(4)]
            rhs = jnp.concatenate([w_ref[k] for k in taps], axis=0)
            part = jnp.dot(lhs, rhs, preferred_element_type=F32)
            acc[i] = part if acc[i] is None else acc[i] + part
    r1 = pltpu.roll(acc[1], 96, 1)
    r2 = pltpu.roll(acc[2], 64, 1)
    r3 = pltpu.roll(acc[3], 32, 1)
    lanes = lax.broadcasted_iota(jnp.int32, acc[0].shape, 1)
    return (jnp.where(lanes < 96, acc[0], r1), jnp.where(lanes < 64, r1, r2), jnp.where(lanes < 32, r2, r3))


def encode_kernel(
    parts, parts2, table, count, send_slot, w_in, wd_in, x_ref,
    enc_ref, out_ref, halo_ref, rot, pooled, face, w_ref, wd_ref, sends, recvs, sends2, recvs2,
):
    step = pl.program_id(0)
    bricks = x_ref.shape[0]
    part = bricks // 4
    size = part // parts
    size2 = part // parts2
    total = bricks + 8 * part
    first = Exchange(
        lambda c: rot.at[0, pl.ds(c * size, size)],
        lambda slot, c: rot.at[0, pl.ds(bricks + slot * part + c * size, size)],
        sends, recvs, parts,
    )
    second = Exchange(
        lambda c: face.at[pl.ds(c * size2, size2)],
        lambda slot, c: halo_ref.at[slot, pl.ds(c * size2, size2)],
        sends2, recvs2, parts2,
    )

    def fill(slot):
        begin = bricks + slot * part
        first.arrive(slot) if OFFSETS[slot][1] else None

        @pl.when(jnp.logical_not(first.has(*OFFSETS[slot])))
        def _():
            def clear(n, carry):
                rot[0, begin + n] = jnp.zeros((3, 16, 128), BF16)
                return carry

            lax.fori_loop(0, part, clear, 0)

        rotate_range(rot, begin, begin + part)

    def densify(start, stop):
        def body(m, carry):
            begin = pl.multiple_of(m * 16, 16)
            x = x_ref[pl.ds(begin, 16)]
            live = lax.broadcasted_iota(jnp.int32, x.shape, 0) + begin < count[0]
            for t, y in enumerate(to_dense(jnp.where(live, x, jnp.zeros((), BF16)))):
                rot[0, pl.ds(begin, 16), t] = y
            return carry

        lax.fori_loop(start // 16, stop // 16, body, 0)

    @pl.when(step == 0)
    def _():
        first.greet()
        densify(0, part)
        first.meet()
        first.start(*range(parts))
        for j in range(4):
            rot[j, total] = jnp.zeros((3, 16, 128), BF16)
        pooled[bricks] = jnp.zeros((8, 128), F32)
        widen(w_ref, w_in)
        chans, half = wd_in.shape[0], wd_in.shape[1] // 2
        for h in range(2):
            side = wd_in[:, h * half : (h + 1) * half].astype(F32)
            side = jnp.concatenate([side, jnp.zeros((128 - chans, half), F32)], axis=0)
            wd_ref[:, h * 128 : (h + 1) * 128] = side.T.astype(BF16)
        densify(part, 2 * part)
        first.forward(0)
        densify(2 * part, 3 * part)
        first.forward(1)
        densify(3 * part, bricks)
        first.forward(2)
        rotate_range(rot, 0, 2 * part)
        first.forward(3)
        rotate_range(rot, 2 * part, bricks)
        first.forward(4)
        fill(3)
        fill(4)
        first.forward(5)
        for slot in (1, 6, 0, 2, 5, 7):
            fill(slot)
        first.finish()

    tiles = conv_block(step, table, w_ref, rot)
    shape = tiles[0].shape
    live = lax.broadcasted_iota(jnp.int32, shape, 0) // 16 + step * BLOCK < count[0]
    values = []
    for u in range(3):
        mine = rot[0, pl.ds(step * BLOCK, BLOCK), u].reshape(shape).astype(F32)
        value = jnp.where(live, mine + jnp.maximum(tiles[u], 0.0), 0.0).astype(BF16)
        enc_ref[:, u] = value.reshape(BLOCK, 16, 128)
        values.append(value)
    sums = jnp.dot(jnp.concatenate(values, axis=1), wd_ref[...], preferred_element_type=F32)
    sums = sums.reshape(BLOCK, 16, 256)
    sums = sums[:, :8, :128] + sums[:, 8:, 128:]
    pooled[pl.ds(step * BLOCK, BLOCK)] = sums

    @pl.when(step == 0)
    def _():
        face[pl.ds(0, BLOCK)] = enc_ref[...]
        second.start(0, 1)

    @pl.when(step == 1)
    def _():
        face[pl.ds(BLOCK, part - BLOCK)] = enc_ref[: part - BLOCK]
        second.start(2)
        second.forward(0)

    @pl.when(step == 2)
    def _():
        second.forward(1)

    @pl.when(step == 3)
    def _():
        second.forward(2)

    @pl.when(step == pl.num_programs(0) - 1)
    def _():
        def place(s, carry):
            out_ref[s] = pooled[send_slot[0, s]].astype(BF16)
            return carry

        lax.fori_loop(0, out_ref.shape[0], place, 0, unroll=8)
        for slot in (0, 2, 3, 4, 5, 7):
            second.arrive(slot)
        second.finish()


def field_scratch(own, halos):
    total = own.shape[0] + len(halos) * halos[0].shape[0]
    return pltpu.VMEM((4, total + 1, 3, 16, 128), BF16)


SMEM = pl.BlockSpec(memory_space=pltpu.SMEM)
VMEM = pl.BlockSpec(memory_space=pltpu.VMEM)
ANY = pl.BlockSpec(memory_space=pl.ANY)


def encode(table, count, send_slot, w, wd, x):
    bricks = x.shape[0]
    part = bricks // 4
    slots = send_slot.shape[1]
    parts, parts2 = 6, 3
    sems = pltpu.SemaphoreType.DMA((8, parts))
    sems2 = pltpu.SemaphoreType.DMA((8, parts2))
    return pl.pallas_call(
        functools.partial(encode_kernel, parts, parts2),
        grid=(bricks // BLOCK,),
        out_shape=(
            jax.ShapeDtypeStruct((bricks, 3, 16, 128), BF16),
            jax.ShapeDtypeStruct((slots, 8, 128), BF16),
            jax.ShapeDtypeStruct((8, part, 3, 16, 128), BF16),
        ),
        in_specs=[SMEM, SMEM, SMEM, VMEM, VMEM, VMEM],
        out_specs=(pl.BlockSpec((BLOCK, 3, 16, 128), lambda i: (i, 0, 0, 0)), VMEM, ANY),
        scratch_shapes=[
            pltpu.VMEM((4, bricks + 8 * part + 1, 3, 16, 128), BF16),
            pltpu.VMEM((bricks + 1, 8, 128), F32),
            pltpu.VMEM((part, 3, 16, 128), BF16),
            pltpu.VMEM((TAPS + 1, 96, 128), BF16),
            pltpu.VMEM((wd.shape[1] // 2, 256), BF16),
            sems, sems, sems2, sems2,
        ],
        compiler_params=pltpu.CompilerParams(
            vmem_limit_bytes=56 * MIB, collective_id=1, has_side_effects=True
        ),
        name="encode",
    )(table, count, send_slot, w, wd, x)


def coarse_mix(from_slot, to_place, w_ref, in_ref, out_ref, cells, grid, turned, mixed):
    places = from_slot.shape[1]
    groups = places // 8

    def land(p, carry):
        cells[pl.ds(pl.multiple_of(p * 8, 8), 8)] = in_ref[from_slot[0, p]].astype(F32)
        return carry

    lax.fori_loop(0, places, land, 0, unroll=8)
    voxels = list(itertools.product(range(4), repeat=3))

    def base(z, y, x):
        t = (z // 2) * 4 + (y // 2) * 2 + x // 2
        c = (z % 2) * 4 + (y % 2) * 2 + x % 2
        return t * places + c

    zero = jnp.zeros((32 - groups, 128), F32)
    for z, y, x in voxels:
        piece = cells[pl.ds(base(z, y, x), groups, stride=8)]
        grid[z + 1, y + 1, x + 1] = jnp.concatenate([piece, zero], axis=0).astype(BF16)

    for z in range(4):
        acc = None
        for k0 in range(0, TAPS + 1, 2):
            sides = []
            for k in (k0, min(k0 + 1, TAPS - 1)):
                dz, dy, dx = k // 9, k // 3 % 3, k % 3
                sides.append(grid[z + dz, dy : dy + 4, dx : dx + 4].reshape(16 * 32, 128))
            rhs = jnp.concatenate([w_ref[k0], w_ref[k0 + 1]], axis=0)
            part = jnp.dot(jnp.concatenate(sides, axis=1), rhs, preferred_element_type=F32)
            acc = part if acc is None else acc + part
        acc = acc.reshape(16, 32, 128)
        for y in range(4):
            for x in range(4):
                here = grid[z + 1, y + 1, x + 1].astype(F32) + jnp.maximum(acc[y * 4 + x], 0.0)
                turned[pl.ds(base(z, y, x), groups, stride=8)] = here[:groups]
    mixed[pl.ds(0, places)] = turned[...].reshape(places, 8, 128)
    mixed[places] = jnp.zeros((8, 128), F32)

    def reply(s, carry):
        out_ref[s] = mixed[to_place[0, s]].astype(BF16)
        return carry

    lax.fori_loop(0, out_ref.shape[0], reply, 0, unroll=8)


def each_peer(act):
    layers, slabs = lax.axis_size("gz"), lax.axis_size("gx")
    devices = layers * slabs
    me = lax.axis_index("gz") * slabs + lax.axis_index("gx")

    def body(i, carry):
        d = (me + i) % devices
        act(d, (d // slabs, d % slabs))
        return carry

    lax.fori_loop(1, devices, body, 0)


class Relay:
    def __init__(self, source, landing, sems):
        self.source, self.landing, self.sems = source, landing, sems
        self.slabs = lax.axis_size("gx")
        self.devices = lax.axis_size("gz") * self.slabs
        self.me = lax.axis_index("gz") * self.slabs + lax.axis_index("gx")
        self.cap = source.shape[0] // self.devices

    def copy(self, begin, end, rows, peer):
        return pltpu.make_async_remote_copy(
            src_ref=self.source.at[pl.ds(begin, rows)],
            dst_ref=self.landing.at[pl.ds(end, rows)],
            send_sem=self.sems.at[0],
            recv_sem=self.sems.at[1],
            device_id=peer,
            device_id_type=MESH,
        )

    def start(self):
        each_peer(lambda d, peer: self.copy(d * self.cap, self.me * self.cap, self.cap, peer).start())
        mine = pl.ds(self.me * self.cap, self.cap)
        self.landing[mine] = self.source[mine]

    def wait(self):
        peer = (self.me + 1) % self.devices
        whole = self.copy(0, 0, self.cap * (self.devices - 1), (peer // self.slabs, peer % self.slabs))
        whole.wait_recv()
        whole.wait_send()


def middle_kernel(
    table, count, from_slot, to_place, slot, w_dec, w_mid, w_up, outgoing, own, halo_ref,
    raw_ref, field, lift, rot, w_ref, wm_ref, stack, wide, incoming, reply, returned,
    cells, grid, turned, mixed, face, landed, local, relays, sends, recvs,
):
    step = pl.program_id(0)
    bricks = own.shape[0]
    part = bricks // 4
    total = bricks + 8 * part
    ring = Exchange(lambda c: face, lambda k, c: landed.at[k], sends, recvs, 1)
    out = Relay(outgoing, incoming, relays.at[0])
    back = Relay(reply, returned, relays.at[1])

    @pl.when(step == 0)
    def _():
        barrier = pltpu.get_barrier_semaphore()
        each_peer(
            lambda d, peer: pl.semaphore_signal(barrier, inc=1, device_id=peer, device_id_type=MESH)
        )
        mine = pltpu.make_async_copy(own, rot.at[0, pl.ds(0, bricks)], local.at[8])
        mine.start()
        piece = lambda k: pltpu.make_async_copy(
            halo_ref.at[k], rot.at[0, pl.ds(bricks + k * part, part)], local.at[k]
        )
        for k in range(8):

            @pl.when(ring.has(*OFFSETS[k]))
            def _():
                piece(k).start()

        pl.semaphore_wait(barrier, out.devices - 1)
        out.start()
        for j in range(4):
            rot[j, total] = jnp.zeros((3, 16, 128), BF16)
        widen(w_ref, w_dec)
        widen(wm_ref, w_mid)
        grid[...] = jnp.zeros(grid.shape, BF16)
        mine.wait()
        rotate_range(rot, 0, bricks)
        for k in range(8):
            here = ring.has(*OFFSETS[k])

            @pl.when(here)
            def _():
                piece(k).wait()

            @pl.when(jnp.logical_not(here))
            def _():
                def clear(n, carry):
                    rot[0, bricks + k * part + n] = jnp.zeros((3, 16, 128), BF16)
                    return carry

                lax.fori_loop(0, part, clear, 0)

        rotate_range(rot, bricks, total)
        merge_weights(w_up, w_dec, lift, stack, wide)
        out.wait()
        coarse_mix(from_slot, to_place, wm_ref, incoming, reply, cells, grid, turned, mixed)
        back.start()

    for u, tile in enumerate(conv_block(step, table, w_ref, rot)):
        raw_ref[:, u] = tile.reshape(BLOCK, 16, 128)

    def take(b, carry):
        value = returned[slot[0, b]].astype(F32)
        field[b] = jnp.where(b < count[0], value, 0.0)
        return carry

    @pl.when(step == 3)
    def _():
        back.wait()
        lax.fori_loop(0, part, take, 0, unroll=8)
        face[...] = field[pl.ds(0, part)].reshape(face.shape).astype(BF16)
        ring.start(0)
        lax.fori_loop(part, bricks, take, 0, unroll=8)
        field[total] = jnp.zeros((8, 128), F32)

    @pl.when(step == 4)
    def _():
        ring.forward(0)

    @pl.when(step == 5)
    def _():
        for k in (3, 4, 1, 6, 0, 2, 5, 7):
            begin = bricks + k * part
            here = ring.has(*OFFSETS[k])
            if OFFSETS[k][1]:
                ring.arrive(k)

            @pl.when(here)
            def _():
                field[pl.ds(begin, part)] = landed[k].astype(F32).reshape(part, 8, 128)

            @pl.when(jnp.logical_not(here))
            def _():
                field[pl.ds(begin, part)] = jnp.zeros((part, 8, 128), F32)

        ring.finish()


def middle(table, count, from_slot, to_place, slot, w_dec, w_mid, w_up, outgoing, own, halos):
    bricks = own.shape[0]
    part = bricks // 4
    total = bricks + 8 * part
    chans = w_up.shape[0]
    places = from_slot.shape[1]
    assert bricks == 6 * BLOCK
    relayed = pltpu.VMEM(outgoing.shape, BF16)
    return pl.pallas_call(
        middle_kernel,
        grid=(bricks // BLOCK,),
        out_shape=(
            jax.ShapeDtypeStruct((bricks, 3, 16, 128), F32),
            jax.ShapeDtypeStruct((total + 1, 8, 128), F32),
            jax.ShapeDtypeStruct((TAPS + 1, 128, 8 * chans), BF16),
        ),
        in_specs=[SMEM] * 5 + [VMEM] * 4 + [ANY, ANY],
        out_specs=(pl.BlockSpec((BLOCK, 3, 16, 128), lambda i: (i, 0, 0, 0)), VMEM, VMEM),
        scratch_shapes=[
            pltpu.VMEM((4, total + 1, 3, 16, 128), BF16),
            pltpu.VMEM((TAPS + 1, 96, 128), BF16),
            pltpu.VMEM((TAPS + 1, 128, 128), BF16),
            pltpu.VMEM((8 * chans, chans), BF16),
            pltpu.VMEM((chans, 128), BF16),
            relayed, relayed, relayed,
            pltpu.VMEM((places * 8, 128), F32),
            pltpu.VMEM((6, 6, 6, 32, 128), BF16),
            pltpu.VMEM((places * 8, 128), F32),
            pltpu.VMEM((places + 1, 8, 128), F32),
            pltpu.VMEM((part // 2, 16, 128), BF16),
            pltpu.VMEM((8, part // 2, 16, 128), BF16),
            pltpu.SemaphoreType.DMA((9,)),
            pltpu.SemaphoreType.DMA((2, 2)),
            pltpu.SemaphoreType.DMA((8, 1)),
            pltpu.SemaphoreType.DMA((8, 1)),
        ],
        compiler_params=pltpu.CompilerParams(
            vmem_limit_bytes=60 * MIB, collective_id=2, has_side_effects=True
        ),
        name="middle",
    )(table, count, from_slot, to_place, slot, w_dec, w_mid, w_up, outgoing, own, halos)


def merge_weights(up_ref, w_in, out_ref, stack, wide):
    chans = up_ref.shape[0]
    out_ref[...] = jnp.zeros(out_ref.shape, BF16)
    wide[...] = jnp.zeros(wide.shape, BF16)
    for s in range(8):
        stack[s * chans : (s + 1) * chans] = up_ref[:, s * chans : (s + 1) * chans]
    lane = lax.broadcasted_iota(jnp.int32, (chans, 128), 1)

    def body(k, carry):
        wide[:, :chans] = w_in[k]
        whole = jnp.dot(stack[...], wide[...], preferred_element_type=F32)
        for h in range(2):
            a = [whole[(4 * h + i) * chans : (4 * h + i + 1) * chans] for i in range(4)]
            r1, r2, r3 = pltpu.roll(a[1], 96, 1), pltpu.roll(a[2], 64, 1), pltpu.roll(a[3], 32, 1)
            tiles = (jnp.where(lane < 96, a[0], r1), jnp.where(lane < 64, r1, r2), jnp.where(lane < 32, r2, r3))
            for u in range(3):
                out_ref[k, :chans, h * 384 + u * 128 : h * 384 + (u + 1) * 128] = tiles[u].astype(BF16)
        return carry

    lax.fori_loop(0, TAPS, body, 0)


def decode_kernel(table, count, w_ref, up_ref, cells, raw_ref, enc_ref, out_ref):
    step = pl.program_id(0)
    block = enc_ref.shape[0]
    acc = None
    for g in range(7):
        columns = []
        for j in range(4):
            k = 4 * g + j
            if k < TAPS:
                rows = [cells[table[k, step * block + b]] for b in range(block)]
                columns.append(jnp.concatenate(rows, axis=0).astype(BF16))
            else:
                columns.append(jnp.zeros((block * 8, 128), BF16))
        lhs = jnp.concatenate(columns, axis=1)
        part_sum = jnp.dot(lhs, w_ref[g * 512 : (g + 1) * 512], preferred_element_type=F32)
        acc = part_sum if acc is None else acc + part_sum
    mine = cells[pl.ds(step * block, block)].reshape(block * 8, 128).astype(BF16)
    up = jnp.concatenate([up_ref[...], jnp.zeros((128 - up_ref.shape[0], up_ref.shape[1]), BF16)], axis=0)
    lifted = jnp.dot(mine, up, preferred_element_type=F32)
    live = lax.broadcasted_iota(jnp.int32, (block, 8, 128), 0) + step * block < count[0]
    tiles = []
    for u in range(3):
        halves = []
        coded = enc_ref[:, u].astype(F32)
        for h in range(2):
            lanes = slice(h * 384 + u * 128, h * 384 + (u + 1) * 128)
            restored = coded[:, h * 8 : h * 8 + 8] + lifted[:, lanes].reshape(block, 8, 128)
            restored = restored.astype(BF16).astype(F32)
            mixed = raw_ref[:, u, h * 8 : h * 8 + 8] + acc[:, lanes].reshape(block, 8, 128)
            halves.append(jnp.where(live, restored + jnp.maximum(mixed, 0.0), 0.0))
        tiles.append(jnp.concatenate(halves, axis=1).astype(BF16))
    for b in range(0, block, 16):
        out_ref[b : b + 16] = from_dense([x[b : b + 16] for x in tiles])


def decode(table, count, w, up, cells, raw, enc, block=48):
    bricks = enc.shape[0]
    blocked = lambda: pl.BlockSpec((block, 3, 16, 128), lambda i: (i, 0, 0, 0))
    return pl.pallas_call(
        decode_kernel,
        grid=(bricks // block,),
        out_shape=jax.ShapeDtypeStruct((bricks, 6144), BF16),
        in_specs=[SMEM, SMEM, VMEM, VMEM, VMEM, blocked(), blocked()],
        out_specs=pl.BlockSpec((block, 6144), lambda i: (i, 0)),
        compiler_params=pltpu.CompilerParams(vmem_limit_bytes=48 * MIB),
        name="decode",
    )(table, count, w, up, cells, raw, enc)


def relay(buffer, devices):
    moved = lax.all_to_all(
        buffer.reshape(devices, -1, 128), ("gz", "gx"), split_axis=0, concat_axis=0, tiled=True
    )
    return moved.reshape(-1, 8, 128)


def route_kernel(cap, owner, arrival, near, send_ref, slot_ref, from_ref, place_ref, table_ref):
    bricks, slots = owner.shape[1], arrival.shape[1]
    part = bricks // 4
    n = near[:, 0]
    m = n - bricks
    moved = jnp.where(m >= 5 * part, n - part, jnp.where(m >= 4 * part, m - 4 * part, n))
    table_ref[...] = jnp.where(n < 0, bricks + 8 * part, moved)
    wide = 256
    row = jnp.concatenate([owner[...].astype(F32), jnp.full((1, wide - bricks), -1.0, F32)], axis=1)
    row = jnp.broadcast_to(row, (wide, wide))
    column = row.T
    down = lax.broadcasted_iota(jnp.int32, (wide, wide), 0)
    across = lax.broadcasted_iota(jnp.int32, (wide, wide), 1)
    same = row == column
    one = lambda x: jnp.where(x, 1.0, 0.0)
    slot_row = row[:1] * cap + jnp.sum(one(same & (down < across)), axis=0, keepdims=True)
    slot_column = column[:, :1] * cap + jnp.sum(one(same & (across < down)), axis=1, keepdims=True)
    slot_ref[...] = slot_row[:, :bricks].astype(jnp.int32)
    ids = lax.broadcasted_iota(jnp.int32, (bricks, slots), 1).astype(F32)
    brick = lax.broadcasted_iota(jnp.int32, (bricks, slots), 0).astype(F32)
    found = jnp.where(slot_column[:bricks] == ids, brick, float(bricks))
    send_ref[...] = jnp.min(found, axis=0, keepdims=True).astype(jnp.int32)
    cell = arrival[...]
    place = jnp.where(cell < 0, bricks, (cell & 7) * (bricks // 8) + (cell >> 3))
    place_ref[...] = place
    turned = jnp.broadcast_to(place.astype(F32), (128, slots)).T[:, :1]
    places = lax.broadcasted_iota(jnp.int32, (slots, bricks), 1).astype(F32)
    source = lax.broadcasted_iota(jnp.int32, (slots, bricks), 0).astype(F32)
    from_ref[...] = jnp.sum(
        jnp.where(turned == places, source, 0.0), axis=0, keepdims=True
    ).astype(jnp.int32)


def route(cap, owner, arrival, near):
    bricks, slots = owner.shape[1], arrival.shape[1]
    one = lambda n: jax.ShapeDtypeStruct((1, n), jnp.int32)
    return pl.pallas_call(
        functools.partial(route_kernel, cap),
        out_shape=(one(slots), one(bricks), one(bricks), one(slots), jax.ShapeDtypeStruct((near.shape[0], bricks), jnp.int32)),
        in_specs=[VMEM, VMEM, VMEM],
        out_specs=(VMEM, VMEM, VMEM, VMEM, VMEM),
        name="route",
    )(owner, arrival, near)


def on_device(
    features, active_count, neighbors, owner, arrival_cell, w_enc, w_down, w_mid, w_up, w_dec
):
    devices = lax.axis_size("gz") * lax.axis_size("gx")
    count = active_count[0]
    near = neighbors.reshape(neighbors.shape[1], 1, neighbors.shape[2])
    send_slot, slot, from_slot, to_place, table = route(
        arrival_cell.shape[1] // devices, owner, arrival_cell, near
    )
    encoded, outgoing, encoded_halo = encode(table, count, send_slot, w_enc, w_down.T, features[0])
    raw, cells, lift = middle(
        table, count, from_slot, to_place, slot, w_dec, w_mid, w_up, outgoing, encoded, encoded_halo
    )
    decoded = decode(table, count, lift.reshape(-1, lift.shape[2]), w_up, cells, raw, encoded)
    return decoded[None]


def solution(mesh):
    placed = (
        P("gz", "gx", None),
        P("gz", "gx"),
        P("gz", None, "gx"),
        P("gz", "gx"),
        P("gz", "gx"),
        P(),
        P(),
        P(),
        P(),
        P(),
    )
    return jax.shard_map(
        on_device, mesh=mesh, in_specs=placed, out_specs=P("gz", "gx", None), check_vma=False
    )
```

```python
import functools
import itertools

import jax
import jax.numpy as jnp
from jax import lax
from jax.experimental import pallas as pl
from jax.experimental.pallas import tpu as pltpu
from jax.sharding import PartitionSpec as P

TAPS = 27
ORDER = [[(q - i) % 4 for q in range(4)] for i in range(4)]
CUT = (96, 64, 32)
BLOCK = 32
CHUNKS = ((0, 1), (2, 3), (4, 5), (6,))
MIB = 1024 * 1024
BF16 = jnp.bfloat16
F32 = jnp.float32


def swap_halves(a, b):
    low = lax.broadcasted_iota(jnp.int32, a[0].shape, a[0].ndim - 1) < 64
    turn = lambda x: pltpu.roll(x, 64, x.ndim - 1)
    a1, a2, b0, b1 = turn(a[1]), turn(a[2]), turn(b[0]), turn(b[1])
    first = (a[0], jnp.where(low, a[1], b0), jnp.where(low, b0, b1))
    second = (jnp.where(low, a1, a2), jnp.where(low, a2, b[1]), b[2])
    return first, second


def group_of(cz, sz, cy):
    return ((cz * 2 + sz) * 2 + cy) * 2, sz * 8 + cz * 4 + cy * 2


def to_dense(x):
    rows = [None] * 16
    for cz, sz, cy in itertools.product(range(2), repeat=3):
        g, r = group_of(cz, sz, cy)
        part = lambda s: [x[:, (g + s) * 384 + t * 128 : (g + s) * 384 + (t + 1) * 128] for t in range(3)]
        rows[r], rows[r + 1] = swap_halves(part(0), part(1))
    return [jnp.swapaxes(jnp.stack([row[t] for row in rows], axis=0), 0, 1) for t in range(3)]


def from_dense(tiles):
    rows = [jnp.swapaxes(x, 0, 1) for x in tiles]
    out = [None] * 16
    for cz, sz, cy in itertools.product(range(2), repeat=3):
        g, r = group_of(cz, sz, cy)
        out[g], out[g + 1] = swap_halves([x[r] for x in rows], [x[r + 1] for x in rows])
    return jnp.concatenate([y for x in out for y in x], axis=1)


OFFSETS = tuple((dz, dx) for dz in (-1, 0, 1) for dx in (-1, 0, 1) if (dz, dx) != (0, 0))
MESH = pl.DeviceIdType.MESH


class Exchange:
    def __init__(self, own, landing, send, recv, chunks, late=()):
        self.own, self.landing, self.send, self.recv, self.chunks = own, landing, send, recv, chunks
        self.late = late
        self.z, self.x = lax.axis_index("gz"), lax.axis_index("gx")
        self.layers, self.slabs = lax.axis_size("gz"), lax.axis_size("gx")

    def has(self, dz, dx):
        checks = []
        if dz:
            checks.append(self.z > 0 if dz < 0 else self.z < self.layers - 1)
        if dx:
            checks.append(self.x > 0 if dx < 0 else self.x < self.slabs - 1)
        return checks[0] if len(checks) == 1 else jnp.logical_and(*checks)

    def sends(self, slot):
        dz, dx = OFFSETS[slot]
        if dz and dx:
            sides = [self.z > 0 if dz < 0 else self.z < self.layers - 1]
            sides.append(self.x < self.slabs - 1 if dx < 0 else self.x > 0)
            return jnp.logical_and(*sides)
        return self.has(-dz, -dx)

    def turns(self, dx):
        return self.x % 2 == (1 if dx > 0 else 0)

    def passes(self, slot, c):
        if c in self.late and all(OFFSETS[slot]):
            return jnp.logical_and(self.sends(slot), self.turns(OFFSETS[slot][1]))
        return self.sends(slot)

    def crosses(self, slot):
        dz, dx = OFFSETS[slot]
        return jnp.logical_and(jnp.logical_and(self.has(0, dx), self.has(-dz, 0)), self.turns(dx))

    def copy(self, slot, c, across=False):
        dz, dx = OFFSETS[slot]
        if across:
            source, target = self.landing(OFFSETS.index((0, dx)), c), (self.z - dz, self.x)
        elif dz and dx:
            source, target = self.landing(OFFSETS.index((dz, 0)), c), (self.z, self.x - dx)
        else:
            source, target = self.own(c), (self.z - dz, self.x - dx)
        return pltpu.make_async_remote_copy(
            src_ref=source,
            dst_ref=self.landing(slot, c),
            send_sem=self.send.at[slot + 8 if across else slot, c],
            recv_sem=self.recv.at[slot, c],
            device_id=target,
            device_id_type=MESH,
        )

    def greet(self):
        barrier = pltpu.get_barrier_semaphore()
        for dz, dx in ((-1, 0), (1, 0), (0, -1), (0, 1)):

            @pl.when(self.has(dz, dx))
            def _():
                pl.semaphore_signal(
                    barrier, inc=1, device_id=(self.z + dz, self.x + dx), device_id_type=MESH
                )

    def meet(self):
        peers = sum(self.has(dz, dx).astype(jnp.int32) for dz, dx in ((-1, 0), (1, 0), (0, -1), (0, 1)))
        pl.semaphore_wait(pltpu.get_barrier_semaphore(), peers)

    def start(self, *chunks):
        for c, d in zip(chunks, chunks[::-1] if self.late and self.late[0] else chunks):
            for slot in (1, 6, 3, 4):

                @pl.when(self.sends(slot))
                def _():
                    self.copy(slot, d if slot in (3, 4) else c).start()

    def forward(self, c):
        for slot, corners in ((1, (0, 2)), (6, (5, 7))):

            @pl.when(self.has(*OFFSETS[slot]))
            def _():
                self.copy(slot, c).wait_recv()

            for corner in corners:

                @pl.when(self.passes(corner, c))
                def _():
                    self.copy(corner, c).start()

    def across(self, c):
        for slot, corners in ((3, (0, 5)), (4, (2, 7))):

            @pl.when(self.has(*OFFSETS[slot]))
            def _():
                self.copy(slot, c).wait_recv()

            for corner in corners:

                @pl.when(self.crosses(corner))
                def _():
                    self.copy(corner, c, True).start()

    def arrive(self, slot):
        @pl.when(self.has(*OFFSETS[slot]))
        def _():
            for c in range(self.chunks):
                if OFFSETS[slot][0] or c not in self.late:
                    self.copy(slot, c).wait_recv()

    def finish(self):
        for slot in range(8):
            for c in range(self.chunks):

                @pl.when(self.passes(slot, c))
                def _():
                    self.copy(slot, c).wait_send()

                if c in self.late and all(OFFSETS[slot]):

                    @pl.when(self.crosses(slot))
                    def _():
                        self.copy(slot, c, True).wait_send()


def rotate_range(rot, start, stop, size=48):
    rows = size * 16
    wide = lax.broadcasted_iota(jnp.int32, (rows, 128), 1)
    source = lax.broadcasted_iota(jnp.int32, (128, 384), 0)
    lane = lax.broadcasted_iota(jnp.int32, (128, 384), 1)
    shift = jnp.where(lane < 128, 96, jnp.where(lane < 256, 64, 32))
    turn = (source == ((lane - shift) & 127)).astype(F32).astype(BF16)

    def body(m, carry):
        n = pl.multiple_of(start + m * size, 16)
        tiles = [rot[0, pl.ds(n, size), t].reshape(rows, 128) for t in range(3)]
        turned = jnp.dot(tiles[0], turn, preferred_element_type=F32).astype(BF16)
        done = []
        for j in range(1, 4):
            amount = (96 * j) % 128
            rolled = [turned[:, (j - 1) * 128 : j * 128]]
            rolled += [pltpu.roll(x, amount, 1) for x in tiles[1:]]
            for u in range(3):
                hi = (128 * u + 127 - 96 * j) // 128 % 3
                lo = (128 * u - 96 * j) // 128 % 3
                done.append((j, u, jnp.where(wide >= amount, rolled[hi], rolled[lo]).reshape(size, 16, 128)))
        for j, u, x in done:
            rot[j, pl.ds(n, size), u] = x
        return carry

    lax.fori_loop(0, (stop - start) // size, body, 0)


def widen(wide, w_ref):
    wide[...] = jnp.zeros(wide.shape, BF16)
    for k in range(w_ref.shape[0]):
        wide[k, : w_ref.shape[1], : w_ref.shape[2]] = w_ref[k]


def conv_block(step, table, w_ref, rot):
    lane = lax.broadcasted_iota(jnp.int32, (16, 128), 1)

    def gather(c, b):
        brick = step * BLOCK + b
        lanes = [[] for _ in range(4)]
        for g in CHUNKS[c]:
            loads = []
            for j in range(4):
                if 4 * g + j < TAPS:
                    n = table[4 * g + j, brick]
                    loads.append([rot[j, n, t] for t in range(3)])
                else:
                    loads.append([jnp.zeros((16, 128), BF16)] * 3)
            for i in range(4):
                for u in range(3):
                    a, b2 = loads[ORDER[i][u]][u], loads[ORDER[i][u + 1]][u]
                    lanes[i].append(jnp.where(lane < CUT[u], a, b2))
        return lanes

    acc = [None] * 4
    for c in range(len(CHUNKS)):
        got = [gather(c, b) for b in range(BLOCK)]
        for i in range(4):
            lhs = jnp.concatenate([jnp.concatenate(x[i], axis=1) for x in got], axis=0)
            taps = [4 * g + ORDER[i][q] for g in CHUNKS[c] for q in range(4)]
            rhs = jnp.concatenate([w_ref[k] for k in taps], axis=0)
            part = jnp.dot(lhs, rhs, preferred_element_type=F32)
            acc[i] = part if acc[i] is None else acc[i] + part
    r1 = pltpu.roll(acc[1], 96, 1)
    r2 = pltpu.roll(acc[2], 64, 1)
    r3 = pltpu.roll(acc[3], 32, 1)
    lanes = lax.broadcasted_iota(jnp.int32, acc[0].shape, 1)
    return (jnp.where(lanes < 96, acc[0], r1), jnp.where(lanes < 64, r1, r2), jnp.where(lanes < 32, r2, r3))


def encode_kernel(
    parts, parts2, table, count, send_slot, w_in, wd_in, x_ref,
    enc_ref, out_ref, halo_ref, rot, pooled, face, w_ref, wd_ref, sends, recvs, sends2, recvs2,
):
    step = pl.program_id(0)
    bricks = x_ref.shape[0]
    part = bricks // 4
    size = part // parts
    size2 = part // parts2
    total = bricks + 8 * part
    first = Exchange(
        lambda c: rot.at[0, pl.ds(c * size, size)],
        lambda slot, c: rot.at[0, pl.ds(bricks + slot * part + c * size, size)],
        sends, recvs, parts, (parts - 1, parts - 2),
    )
    second = Exchange(
        lambda c: face.at[pl.ds(c * size2, size2)],
        lambda slot, c: halo_ref.at[slot, pl.ds(c * size2, size2)],
        sends2, recvs2, parts2, (0,),
    )

    def fill(slot):
        begin = bricks + slot * part
        first.arrive(slot) if OFFSETS[slot][1] else None

        @pl.when(jnp.logical_not(first.has(*OFFSETS[slot])))
        def _():
            def clear(n, carry):
                rot[0, begin + n] = jnp.zeros((3, 16, 128), BF16)
                return carry

            lax.fori_loop(0, part, clear, 0)

        rotate_range(rot, begin, begin + part)

    def densify(start, stop):
        def body(m, carry):
            begin = pl.multiple_of(m * 16, 16)
            x = x_ref[pl.ds(begin, 16)]
            live = lax.broadcasted_iota(jnp.int32, x.shape, 0) + begin < count[0]
            for t, y in enumerate(to_dense(jnp.where(live, x, jnp.zeros((), BF16)))):
                rot[0, pl.ds(begin, 16), t] = y
            return carry

        lax.fori_loop(start // 16, stop // 16, body, 0)

    @pl.when(step == 0)
    def _():
        first.greet()
        densify(0, part)
        first.meet()
        first.start(*range(parts))
        for j in range(4):
            rot[j, total] = jnp.zeros((3, 16, 128), BF16)
        pooled[bricks] = jnp.zeros((8, 128), F32)
        widen(w_ref, w_in)
        chans, half = wd_in.shape[0], wd_in.shape[1] // 2
        for h in range(2):
            side = wd_in[:, h * half : (h + 1) * half].astype(F32)
            side = jnp.concatenate([side, jnp.zeros((128 - chans, half), F32)], axis=0)
            wd_ref[:, h * 128 : (h + 1) * 128] = side.T.astype(BF16)
        densify(part, 2 * part)
        first.forward(0)
        densify(2 * part, 3 * part)
        first.forward(1)
        first.across(5)
        first.across(4)
        densify(3 * part, bricks)
        first.forward(2)
        rotate_range(rot, 0, 2 * part)
        first.forward(3)
        rotate_range(rot, 2 * part, bricks)
        first.forward(4)
        fill(3)
        fill(4)
        first.forward(5)
        for slot in (1, 6, 0, 2, 5, 7):
            fill(slot)
        first.finish()

    tiles = conv_block(step, table, w_ref, rot)
    shape = tiles[0].shape
    live = lax.broadcasted_iota(jnp.int32, shape, 0) // 16 + step * BLOCK < count[0]
    values = []
    for u in range(3):
        mine = rot[0, pl.ds(step * BLOCK, BLOCK), u].reshape(shape).astype(F32)
        value = jnp.where(live, mine + jnp.maximum(tiles[u], 0.0), 0.0).astype(BF16)
        enc_ref[:, u] = value.reshape(BLOCK, 16, 128)
        values.append(value)
    sums = jnp.dot(jnp.concatenate(values, axis=1), wd_ref[...], preferred_element_type=F32)
    sums = sums.reshape(BLOCK, 16, 256)
    sums = sums[:, :8, :128] + sums[:, 8:, 128:]
    pooled[pl.ds(step * BLOCK, BLOCK)] = sums

    @pl.when(step == 0)
    def _():
        face[pl.ds(0, BLOCK)] = enc_ref[...]
        second.start(0, 1)

    @pl.when(step == 1)
    def _():
        face[pl.ds(BLOCK, part - BLOCK)] = enc_ref[: part - BLOCK]
        second.start(2)
        second.forward(0)
        second.across(0)

    @pl.when(step == 2)
    def _():
        second.forward(1)

    @pl.when(step == 3)
    def _():
        second.forward(2)

    @pl.when(step == pl.num_programs(0) - 1)
    def _():
        def place(s, carry):
            out_ref[s] = pooled[send_slot[0, s]].astype(BF16)
            return carry

        lax.fori_loop(0, out_ref.shape[0], place, 0, unroll=8)
        for slot in (0, 2, 3, 4, 5, 7):
            second.arrive(slot)
        second.finish()


def field_scratch(own, halos):
    total = own.shape[0] + len(halos) * halos[0].shape[0]
    return pltpu.VMEM((4, total + 1, 3, 16, 128), BF16)


SMEM = pl.BlockSpec(memory_space=pltpu.SMEM)
VMEM = pl.BlockSpec(memory_space=pltpu.VMEM)
ANY = pl.BlockSpec(memory_space=pl.ANY)


def encode(table, count, send_slot, w, wd, x):
    bricks = x.shape[0]
    part = bricks // 4
    slots = send_slot.shape[1]
    parts, parts2 = 6, 3
    sems = pltpu.SemaphoreType.DMA((16, parts))
    sems2 = pltpu.SemaphoreType.DMA((16, parts2))
    return pl.pallas_call(
        functools.partial(encode_kernel, parts, parts2),
        grid=(bricks // BLOCK,),
        out_shape=(
            jax.ShapeDtypeStruct((bricks, 3, 16, 128), BF16),
            jax.ShapeDtypeStruct((slots, 8, 128), BF16),
            jax.ShapeDtypeStruct((8, part, 3, 16, 128), BF16),
        ),
        in_specs=[SMEM, SMEM, SMEM, VMEM, VMEM, VMEM],
        out_specs=(pl.BlockSpec((BLOCK, 3, 16, 128), lambda i: (i, 0, 0, 0)), VMEM, ANY),
        scratch_shapes=[
            pltpu.VMEM((4, bricks + 8 * part + 1, 3, 16, 128), BF16),
            pltpu.VMEM((bricks + 1, 8, 128), F32),
            pltpu.VMEM((part, 3, 16, 128), BF16),
            pltpu.VMEM((TAPS + 1, 96, 128), BF16),
            pltpu.VMEM((wd.shape[1] // 2, 256), BF16),
            sems, sems, sems2, sems2,
        ],
        compiler_params=pltpu.CompilerParams(
            vmem_limit_bytes=56 * MIB, collective_id=1, has_side_effects=True
        ),
        name="encode",
    )(table, count, send_slot, w, wd, x)


def coarse_mix(from_slot, to_place, w_ref, in_ref, out_ref, cells, grid, turned, mixed):
    places = from_slot.shape[1]
    groups = places // 8

    def land(p, carry):
        cells[pl.ds(pl.multiple_of(p * 8, 8), 8)] = in_ref[from_slot[0, p]].astype(F32)
        return carry

    lax.fori_loop(0, places, land, 0, unroll=8)
    voxels = list(itertools.product(range(4), repeat=3))

    def base(z, y, x):
        t = (z // 2) * 4 + (y // 2) * 2 + x // 2
        c = (z % 2) * 4 + (y % 2) * 2 + x % 2
        return t * places + c

    zero = jnp.zeros((32 - groups, 128), F32)
    for z, y, x in voxels:
        piece = cells[pl.ds(base(z, y, x), groups, stride=8)]
        grid[z + 1, y + 1, x + 1] = jnp.concatenate([piece, zero], axis=0).astype(BF16)

    for z in range(4):
        acc = None
        for k0 in range(0, TAPS + 1, 2):
            sides = []
            for k in (k0, min(k0 + 1, TAPS - 1)):
                dz, dy, dx = k // 9, k // 3 % 3, k % 3
                sides.append(grid[z + dz, dy : dy + 4, dx : dx + 4].reshape(16 * 32, 128))
            rhs = jnp.concatenate([w_ref[k0], w_ref[k0 + 1]], axis=0)
            part = jnp.dot(jnp.concatenate(sides, axis=1), rhs, preferred_element_type=F32)
            acc = part if acc is None else acc + part
        acc = acc.reshape(16, 32, 128)
        for y in range(4):
            for x in range(4):
                here = grid[z + 1, y + 1, x + 1].astype(F32) + jnp.maximum(acc[y * 4 + x], 0.0)
                turned[pl.ds(base(z, y, x), groups, stride=8)] = here[:groups]
    mixed[pl.ds(0, places)] = turned[...].reshape(places, 8, 128)
    mixed[places] = jnp.zeros((8, 128), F32)

    def reply(s, carry):
        out_ref[s] = mixed[to_place[0, s]].astype(BF16)
        return carry

    lax.fori_loop(0, out_ref.shape[0], reply, 0, unroll=8)


def each_peer(act):
    layers, slabs = lax.axis_size("gz"), lax.axis_size("gx")
    devices = layers * slabs
    me = lax.axis_index("gz") * slabs + lax.axis_index("gx")

    def body(i, carry):
        d = (me + i) % devices
        act(d, (d // slabs, d % slabs))
        return carry

    lax.fori_loop(1, devices, body, 0)


class Relay:
    def __init__(self, source, landing, sems):
        self.source, self.landing, self.sems = source, landing, sems
        self.slabs = lax.axis_size("gx")
        self.devices = lax.axis_size("gz") * self.slabs
        self.me = lax.axis_index("gz") * self.slabs + lax.axis_index("gx")
        self.cap = source.shape[0] // self.devices

    def copy(self, begin, end, rows, peer):
        return pltpu.make_async_remote_copy(
            src_ref=self.source.at[pl.ds(begin, rows)],
            dst_ref=self.landing.at[pl.ds(end, rows)],
            send_sem=self.sems.at[0],
            recv_sem=self.sems.at[1],
            device_id=peer,
            device_id_type=MESH,
        )

    def start(self):
        each_peer(lambda d, peer: self.copy(d * self.cap, self.me * self.cap, self.cap, peer).start())
        mine = pl.ds(self.me * self.cap, self.cap)
        self.landing[mine] = self.source[mine]

    def wait(self):
        peer = (self.me + 1) % self.devices
        whole = self.copy(0, 0, self.cap * (self.devices - 1), (peer // self.slabs, peer % self.slabs))
        whole.wait_recv()
        whole.wait_send()


def middle_kernel(
    table, count, from_slot, to_place, slot, w_dec, w_mid, w_up, outgoing, own, halo_ref,
    raw_ref, field, lift_out, rot, lift, w_ref, wm_ref, stack, wide, incoming, reply, returned,
    cells, grid, turned, mixed, face, landed, local, relays, sends, recvs,
):
    step = pl.program_id(0)
    bricks = own.shape[0]
    part = bricks // 4
    total = bricks + 8 * part
    ring = Exchange(lambda c: face, lambda k, c: landed.at[k], sends, recvs, 1)
    out = Relay(outgoing, incoming, relays.at[0])
    back = Relay(reply, returned, relays.at[1])

    @pl.when(step == 0)
    def _():
        barrier = pltpu.get_barrier_semaphore()
        each_peer(
            lambda d, peer: pl.semaphore_signal(barrier, inc=1, device_id=peer, device_id_type=MESH)
        )
        mine = pltpu.make_async_copy(own, rot.at[0, pl.ds(0, bricks)], local.at[8])
        mine.start()
        piece = lambda k: pltpu.make_async_copy(
            halo_ref.at[k], rot.at[0, pl.ds(bricks + k * part, part)], local.at[k]
        )
        for k in range(8):

            @pl.when(ring.has(*OFFSETS[k]))
            def _():
                piece(k).start()

        pl.semaphore_wait(barrier, out.devices - 1)
        out.start()
        for j in range(4):
            rot[j, total] = jnp.zeros((3, 16, 128), BF16)
        widen(w_ref, w_dec)
        widen(wm_ref, w_mid)
        grid[...] = jnp.zeros(grid.shape, BF16)
        mine.wait()
        rotate_range(rot, 0, bricks)
        for k in range(8):
            here = ring.has(*OFFSETS[k])

            @pl.when(here)
            def _():
                piece(k).wait()

            @pl.when(jnp.logical_not(here))
            def _():
                def clear(n, carry):
                    rot[0, bricks + k * part + n] = jnp.zeros((3, 16, 128), BF16)
                    return carry

                lax.fori_loop(0, part, clear, 0)

        rotate_range(rot, bricks, total)
        merge_weights(w_up, w_dec, lift, stack, wide)
        pltpu.make_async_copy(lift, lift_out, local.at[9]).start()
        out.wait()
        coarse_mix(from_slot, to_place, wm_ref, incoming, reply, cells, grid, turned, mixed)
        back.start()

    for u, tile in enumerate(conv_block(step, table, w_ref, rot)):
        raw_ref[:, u] = tile.reshape(BLOCK, 16, 128)

    def take(b, carry):
        value = returned[slot[0, b]].astype(F32)
        field[b] = jnp.where(b < count[0], value, 0.0)
        return carry

    @pl.when(step == 3)
    def _():
        back.wait()
        lax.fori_loop(0, part, take, 0, unroll=8)
        face[...] = field[pl.ds(0, part)].reshape(face.shape).astype(BF16)
        ring.start(0)
        lax.fori_loop(part, bricks, take, 0, unroll=8)
        field[total] = jnp.zeros((8, 128), F32)

    @pl.when(step == 4)
    def _():
        ring.forward(0)

    @pl.when(step == 5)
    def _():
        for k in (3, 4, 1, 6, 0, 2, 5, 7):
            begin = bricks + k * part
            here = ring.has(*OFFSETS[k])
            if OFFSETS[k][1]:
                ring.arrive(k)

            @pl.when(here)
            def _():
                field[pl.ds(begin, part)] = landed[k].astype(F32).reshape(part, 8, 128)

            @pl.when(jnp.logical_not(here))
            def _():
                field[pl.ds(begin, part)] = jnp.zeros((part, 8, 128), F32)

        ring.finish()
        pltpu.make_async_copy(lift, lift_out, local.at[9]).wait()


def middle(table, count, from_slot, to_place, slot, w_dec, w_mid, w_up, outgoing, own, halos):
    bricks = own.shape[0]
    part = bricks // 4
    total = bricks + 8 * part
    chans = w_up.shape[0]
    places = from_slot.shape[1]
    assert bricks == 6 * BLOCK
    relayed = pltpu.VMEM(outgoing.shape, BF16)
    return pl.pallas_call(
        middle_kernel,
        grid=(bricks // BLOCK,),
        out_shape=(
            jax.ShapeDtypeStruct((bricks, 3, 16, 128), F32),
            jax.ShapeDtypeStruct((total + 1, 8, 128), F32),
            jax.ShapeDtypeStruct((TAPS + 1, 128, 8 * chans), BF16),
        ),
        in_specs=[SMEM] * 5 + [VMEM] * 4 + [ANY, ANY],
        out_specs=(pl.BlockSpec((BLOCK, 3, 16, 128), lambda i: (i, 0, 0, 0)), VMEM, ANY),
        scratch_shapes=[
            pltpu.VMEM((4, total + 1, 3, 16, 128), BF16),
            pltpu.VMEM((TAPS + 1, 128, 8 * chans), BF16),
            pltpu.VMEM((TAPS + 1, 96, 128), BF16),
            pltpu.VMEM((TAPS + 1, 128, 128), BF16),
            pltpu.VMEM((8 * chans, chans), BF16),
            pltpu.VMEM((chans, 128), BF16),
            relayed, relayed, relayed,
            pltpu.VMEM((places * 8, 128), F32),
            pltpu.VMEM((6, 6, 6, 32, 128), BF16),
            pltpu.VMEM((places * 8, 128), F32),
            pltpu.VMEM((places + 1, 8, 128), F32),
            pltpu.VMEM((part // 2, 16, 128), BF16),
            pltpu.VMEM((8, part // 2, 16, 128), BF16),
            pltpu.SemaphoreType.DMA((10,)),
            pltpu.SemaphoreType.DMA((2, 2)),
            pltpu.SemaphoreType.DMA((8, 1)),
            pltpu.SemaphoreType.DMA((8, 1)),
        ],
        compiler_params=pltpu.CompilerParams(
            vmem_limit_bytes=60 * MIB, collective_id=2, has_side_effects=True
        ),
        name="middle",
    )(table, count, from_slot, to_place, slot, w_dec, w_mid, w_up, outgoing, own, halos)


def merge_weights(up_ref, w_in, out_ref, stack, wide):
    chans = up_ref.shape[0]
    out_ref[...] = jnp.zeros(out_ref.shape, BF16)
    wide[...] = jnp.zeros(wide.shape, BF16)
    for s in range(8):
        stack[s * chans : (s + 1) * chans] = up_ref[:, s * chans : (s + 1) * chans]
    lane = lax.broadcasted_iota(jnp.int32, (chans, 128), 1)

    def body(k, carry):
        wide[:, :chans] = w_in[k]
        whole = jnp.dot(stack[...], wide[...], preferred_element_type=F32)
        for h in range(2):
            a = [whole[(4 * h + i) * chans : (4 * h + i + 1) * chans] for i in range(4)]
            r1, r2, r3 = pltpu.roll(a[1], 96, 1), pltpu.roll(a[2], 64, 1), pltpu.roll(a[3], 32, 1)
            tiles = (jnp.where(lane < 96, a[0], r1), jnp.where(lane < 64, r1, r2), jnp.where(lane < 32, r2, r3))
            for u in range(3):
                out_ref[k, :chans, h * 384 + u * 128 : h * 384 + (u + 1) * 128] = tiles[u].astype(BF16)
        return carry

    lax.fori_loop(0, TAPS, body, 0)


def decode_kernel(table, count, w_ref, up_ref, cells, raw_ref, enc_ref, out_ref):
    step = pl.program_id(0)
    block = enc_ref.shape[0]
    acc = None
    for g in range(7):
        columns = []
        for j in range(4):
            k = 4 * g + j
            if k < TAPS:
                rows = [cells[table[k, step * block + b]] for b in range(block)]
                columns.append(jnp.concatenate(rows, axis=0).astype(BF16))
            else:
                columns.append(jnp.zeros((block * 8, 128), BF16))
        lhs = jnp.concatenate(columns, axis=1)
        part_sum = jnp.dot(lhs, w_ref[g * 512 : (g + 1) * 512], preferred_element_type=F32)
        acc = part_sum if acc is None else acc + part_sum
    mine = cells[pl.ds(step * block, block)].reshape(block * 8, 128).astype(BF16)
    up = jnp.concatenate([up_ref[...], jnp.zeros((128 - up_ref.shape[0], up_ref.shape[1]), BF16)], axis=0)
    lifted = jnp.dot(mine, up, preferred_element_type=F32)
    live = lax.broadcasted_iota(jnp.int32, (block, 8, 128), 0) + step * block < count[0]
    tiles = []
    for u in range(3):
        halves = []
        coded = enc_ref[:, u].astype(F32)
        for h in range(2):
            lanes = slice(h * 384 + u * 128, h * 384 + (u + 1) * 128)
            restored = coded[:, h * 8 : h * 8 + 8] + lifted[:, lanes].reshape(block, 8, 128)
            restored = restored.astype(BF16).astype(F32)
            mixed = raw_ref[:, u, h * 8 : h * 8 + 8] + acc[:, lanes].reshape(block, 8, 128)
            halves.append(jnp.where(live, restored + jnp.maximum(mixed, 0.0), 0.0))
        tiles.append(jnp.concatenate(halves, axis=1).astype(BF16))
    for b in range(0, block, 16):
        out_ref[b : b + 16] = from_dense([x[b : b + 16] for x in tiles])


def decode(table, count, w, up, cells, raw, enc, block=48):
    bricks = enc.shape[0]
    blocked = lambda: pl.BlockSpec((block, 3, 16, 128), lambda i: (i, 0, 0, 0))
    return pl.pallas_call(
        decode_kernel,
        grid=(bricks // block,),
        out_shape=jax.ShapeDtypeStruct((bricks, 6144), BF16),
        in_specs=[SMEM, SMEM, VMEM, VMEM, VMEM, blocked(), blocked()],
        out_specs=pl.BlockSpec((block, 6144), lambda i: (i, 0)),
        compiler_params=pltpu.CompilerParams(vmem_limit_bytes=48 * MIB),
        name="decode",
    )(table, count, w, up, cells, raw, enc)


def relay(buffer, devices):
    moved = lax.all_to_all(
        buffer.reshape(devices, -1, 128), ("gz", "gx"), split_axis=0, concat_axis=0, tiled=True
    )
    return moved.reshape(-1, 8, 128)


def route_kernel(cap, owner, arrival, near, send_ref, slot_ref, from_ref, place_ref, table_ref):
    bricks, slots = owner.shape[1], arrival.shape[1]
    part = bricks // 4
    n = near[:, 0]
    m = n - bricks
    moved = jnp.where(m >= 5 * part, n - part, jnp.where(m >= 4 * part, m - 4 * part, n))
    table_ref[...] = jnp.where(n < 0, bricks + 8 * part, moved)
    wide = 256
    row = jnp.concatenate([owner[...].astype(F32), jnp.full((1, wide - bricks), -1.0, F32)], axis=1)
    row = jnp.broadcast_to(row, (wide, wide))
    column = row.T
    down = lax.broadcasted_iota(jnp.int32, (wide, wide), 0)
    across = lax.broadcasted_iota(jnp.int32, (wide, wide), 1)
    same = row == column
    one = lambda x: jnp.where(x, 1.0, 0.0)
    slot_row = row[:1] * cap + jnp.sum(one(same & (down < across)), axis=0, keepdims=True)
    slot_column = column[:, :1] * cap + jnp.sum(one(same & (across < down)), axis=1, keepdims=True)
    slot_ref[...] = slot_row[:, :bricks].astype(jnp.int32)
    ids = lax.broadcasted_iota(jnp.int32, (bricks, slots), 1).astype(F32)
    brick = lax.broadcasted_iota(jnp.int32, (bricks, slots), 0).astype(F32)
    found = jnp.where(slot_column[:bricks] == ids, brick, float(bricks))
    send_ref[...] = jnp.min(found, axis=0, keepdims=True).astype(jnp.int32)
    cell = arrival[...]
    place = jnp.where(cell < 0, bricks, (cell & 7) * (bricks // 8) + (cell >> 3))
    place_ref[...] = place
    turned = jnp.broadcast_to(place.astype(F32), (128, slots)).T[:, :1]
    places = lax.broadcasted_iota(jnp.int32, (slots, bricks), 1).astype(F32)
    source = lax.broadcasted_iota(jnp.int32, (slots, bricks), 0).astype(F32)
    from_ref[...] = jnp.sum(
        jnp.where(turned == places, source, 0.0), axis=0, keepdims=True
    ).astype(jnp.int32)


def route(cap, owner, arrival, near):
    bricks, slots = owner.shape[1], arrival.shape[1]
    one = lambda n: jax.ShapeDtypeStruct((1, n), jnp.int32)
    return pl.pallas_call(
        functools.partial(route_kernel, cap),
        out_shape=(one(slots), one(bricks), one(bricks), one(slots), jax.ShapeDtypeStruct((near.shape[0], bricks), jnp.int32)),
        in_specs=[VMEM, VMEM, VMEM],
        out_specs=(VMEM, VMEM, VMEM, VMEM, VMEM),
        name="route",
    )(owner, arrival, near)


def on_device(
    features, active_count, neighbors, owner, arrival_cell, w_enc, w_down, w_mid, w_up, w_dec
):
    devices = lax.axis_size("gz") * lax.axis_size("gx")
    count = active_count[0]
    near = neighbors.reshape(neighbors.shape[1], 1, neighbors.shape[2])
    send_slot, slot, from_slot, to_place, table = route(
        arrival_cell.shape[1] // devices, owner, arrival_cell, near
    )
    encoded, outgoing, encoded_halo = encode(table, count, send_slot, w_enc, w_down.T, features[0])
    raw, cells, lift = middle(
        table, count, from_slot, to_place, slot, w_dec, w_mid, w_up, outgoing, encoded, encoded_halo
    )
    decoded = decode(table, count, lift.reshape(-1, lift.shape[2]), w_up, cells, raw, encoded)
    return decoded[None]


def solution(mesh):
    placed = (
        P("gz", "gx", None),
        P("gz", "gx"),
        P("gz", None, "gx"),
        P("gz", "gx"),
        P("gz", "gx"),
        P(),
        P(),
        P(),
        P(),
        P(),
    )
    return jax.shard_map(
        on_device, mesh=mesh, in_specs=placed, out_specs=P("gz", "gx", None), check_vma=False
    )
```
